512 devices in a mesh: st: 128 (over z, x, y_lo), tb: 4 (over y_hi, core).
Axes of the slice: x: 4, y: 8 (y_hi: 2, y_lo: 4; y = y_hi * 4 + y_lo), z: 8, core: 2. Of those that a mesh axis runs over, the one named last changes fastest.
Arguments:
- voltages: bfloat16 [1024, 98304], P('st', 'tb'), may hold values from -6 to 6
- fir_taps: float32 [12, 512], replicated, may hold values from -1.75 to 1.75
Outputs:
- visibilities: float32 [2, 128, 1024, 1024], P(None, 'st', 'tb')
The draws below stay inside these ranges and needn't reach their ends.
All inputs are finite; a program needn't handle non-finite values.
Results may differ from the reference program's by a relative error of at most 0.0037.
Values may be sent and summed in bfloat16 or wider, within the bound.
No kernel may reach another device: no remote copies, remote signals or barrier semaphores. Data moves between devices by JAX's collectives and lax.ppermute only.
A program may use at most 64 MiB of HBM per device.

```python
import math
import jax
import jax.numpy as jnp
from jax import lax

INPUTS = 1024
FRAME = 512
CH = 128
TAPS = 12
FRAMES = 192
SAMPLES = 98304
OFFSET = 64


def steps_of(stream_key, shape, shards, low, high):
    loudness, own = 1.0, jax.random.fold_in(stream_key, 6)
    for position, parts in shards:
        steps = jnp.exp(jax.random.uniform(jax.random.fold_in(own, position), (parts,), jnp.float32, low / len(shards), high / len(shards)))
        loudness = loudness * jnp.repeat(steps, shape[position] // parts).reshape([-1 if axis == position else 1 for axis in range(len(shape))])
    return loudness


def bell_draw(own_key, shape, deviation, reach, pieces=(), kind=jnp.bfloat16):
    loudness = steps_of(own_key, shape, pieces, -0.22, 0.18) if pieces else 1.0
    values = jax.random.normal(own_key, shape, jnp.float32) * deviation * loudness
    return jnp.minimum(jnp.maximum(values, -reach), reach).astype(kind)


def setup_inputs(seed: int = 0) -> dict:
    key_list = jax.random.split(jax.random.key(seed), 3)
    return {
        "voltages": bell_draw(key_list[0], (INPUTS, SAMPLES), 1.0, 6.0, ((0, 128), (1, 4))),
        "fir_taps": bell_draw(key_list[1], (TAPS, FRAME), TAPS ** -0.5, 1.75, (), jnp.float32),
    }


def reference(voltages, fir_taps):

    def channelize(group):
        count = group.shape[0]
        frames = group.reshape(count, FRAMES, FRAME)
        padded = jnp.concatenate([jnp.zeros((count, TAPS - 1, FRAME), jnp.bfloat16), frames], 1)
        filtered = jnp.zeros((count, FRAMES, FRAME), jnp.float32)
        for tap in range(TAPS):
            filtered = filtered + fir_taps[tap] * padded[:, tap:tap + FRAMES, :].astype(jnp.float32)
        spectrum = jnp.fft.rfft(filtered, axis=2)[:, :, OFFSET:OFFSET + CH]
        real_part = (jnp.real(spectrum) / math.sqrt(FRAME)).astype(jnp.bfloat16)
        imag_part = (jnp.imag(spectrum) / math.sqrt(FRAME)).astype(jnp.bfloat16)
        return jnp.stack([real_part, imag_part], 2)
    groups = voltages.reshape(INPUTS // 64, 64, SAMPLES)
    spectra = lax.map(channelize, groups).reshape(INPUTS, FRAMES, 2, CH)
    rotated = jnp.stack([-spectra[:, :, 1], spectra[:, :, 0]], 2)
    spectra_c = jnp.moveaxis(spectra, 3, 0)
    rotated_c = jnp.moveaxis(rotated, 3, 0)

    def correlate(pair):
        plain = pair[0].reshape(INPUTS, FRAMES * 2)
        turned = pair[1].reshape(INPUTS, FRAMES * 2)
        real_vis = jnp.dot(plain, plain.T, preferred_element_type=jnp.float32)
        imag_vis = jnp.dot(plain, turned.T, preferred_element_type=jnp.float32)
        return jnp.stack([real_vis, imag_vis], 0)
    result = lax.map(correlate, (spectra_c, rotated_c))
    return jnp.transpose(result, (1, 0, 2, 3)) / jnp.float32(FRAMES)
```

```python
import math

import jax
import jax.numpy as jnp
import numpy as np
from jax import lax
from jax.experimental import pallas as pl
from jax.experimental.pallas import tpu as pltpu
from jax.sharding import Mesh
from jax.sharding import PartitionSpec as P

CH = 128
OFFSET = 64
FRAME = 512
TAPS = 12
N_IN = 8
N_FR = 48
N_TB = 4
N_ZX = 32
N_Y = 4
PIECE = 2 * N_FR
WIDTH = N_Y * PIECE
LANES = 128
VMEM = pl.BlockSpec(memory_space=pltpu.VMEM)
PARAMS = pltpu.CompilerParams(vmem_limit_bytes=40 * 1024 * 1024)


def dft_tables():
    ylo = np.arange(N_Y)[:, None, None]
    part = np.arange(2)[None, :, None]
    zx = np.arange(N_ZX)[None, None, :]
    channel = (zx * N_Y + ylo + 0 * part).reshape(-1) + OFFSET
    is_im = (part + 0 * ylo + 0 * zx).reshape(-1)
    phase = channel[:, None] * np.arange(FRAME)[None, :] % FRAME
    angle = phase * (2.0 * math.pi / FRAME)
    table = np.where(is_im[:, None] == 1, -np.sin(angle), np.cos(angle)) / math.sqrt(FRAME)
    high = table.astype(jnp.bfloat16)
    low = (table - high.astype(np.float64)).astype(jnp.bfloat16)
    return high, low


def lane_ids(rows):
    return lax.broadcasted_iota(jnp.int32, (rows, LANES), 1)


def turned(block, shift):
    shift %= LANES
    return block if shift == 0 else pltpu.roll(block, shift, 1)


def dot_t(a, b):
    return lax.dot_general(a, b, (((1,), (1,)), ((), ())), preferred_element_type=jnp.float32)


def channelize_kernel(halo_ref, volt_ref, taps_ref, high_ref, low_ref, out_ref, filt, fhigh, flow, spread):
    margin = TAPS - 1
    for block in range(FRAME // LANES):
        lo = block * LANES
        taps = [jnp.broadcast_to(taps_ref[k : k + 1, lo : lo + LANES], (N_IN, LANES)) for k in range(TAPS)]
        window = []
        for t in range(N_FR + margin):
            if t < margin:
                v = halo_ref[:, t * FRAME + lo : t * FRAME + lo + LANES]
            else:
                v = volt_ref[:, (t - margin) * FRAME + lo : (t - margin) * FRAME + lo + LANES]
            window.append(v.astype(jnp.float32))
            if t < margin:
                continue
            total = taps[0] * window[0]
            for k in range(1, TAPS):
                total = total + taps[k] * window[k]
            window.pop(0)
            f = t - margin
            filt[block, f * N_IN : (f + 1) * N_IN, :] = total
    for i in range(N_IN):
        for block in range(FRAME // LANES):
            lo = block * LANES
            x = filt[block, pl.ds(i, N_FR, stride=N_IN), :]
            high = x.astype(jnp.bfloat16)
            low = (x - high.astype(jnp.float32)).astype(jnp.bfloat16)
            fhigh[i * 64 : i * 64 + N_FR, lo : lo + LANES] = high
            flow[i * 64 : i * 64 + N_FR, lo : lo + LANES] = low
        zero = jnp.zeros((64 - N_FR, FRAME), jnp.bfloat16)
        fhigh[i * 64 + N_FR : (i + 1) * 64, :] = zero
        flow[i * 64 + N_FR : (i + 1) * 64, :] = zero
    lanes = lane_ids(N_ZX)
    for pair in range(N_IN // 2):
        fh = fhigh[pair * LANES : (pair + 1) * LANES, :]
        fl = flow[pair * LANES : (pair + 1) * LANES, :]
        spec = dot_t(high_ref[...], fh) + (dot_t(high_ref[...], fl) + dot_t(low_ref[...], fh))
        for sub in range(2):
            i = pair * 2 + sub
            tiles = [jnp.zeros((N_ZX, LANES), jnp.float32) for _ in range(WIDTH // LANES)]
            for j in range(2 * N_Y):
                rows = spec[j * N_ZX : (j + 1) * N_ZX, :]
                start = j * N_FR
                rolled = turned(rows, start - sub * 64)
                for t in range(start // LANES, (start + N_FR - 1) // LANES + 1):
                    first = max(start - t * LANES, 0)
                    last = min(start + N_FR - t * LANES, LANES)
                    tiles[t] = jnp.where((lanes >= first) & (lanes < last), rolled, tiles[t])
            for t in range(WIDTH // LANES):
                spread[t, pl.ds(i, N_ZX, stride=N_IN), :] = tiles[t]
    for t in range(WIDTH // LANES):
        out_ref[:, t * LANES : (t + 1) * LANES] = spread[t].astype(jnp.bfloat16)


def move_lanes(sources, start, width, to, tiles, lanes):
    done = 0
    while done < width:
        src, dst = start + done, to + done
        n = min(width - done, LANES - src % LANES, LANES - dst % LANES)
        t = dst // LANES
        rolled = turned(sources[src // LANES], dst - src)
        first = dst % LANES
        if n == LANES:
            tiles[t] = rolled
        else:
            tiles[t] = jnp.where((lanes >= first) & (lanes < first + n), rolled, tiles[t])
        done += n


def repack_kernel(in_ref, out_ref):
    rows = 64
    lanes = lane_ids(rows)
    n_tiles = WIDTH // LANES
    zero = jnp.zeros((rows, LANES), jnp.float32)
    data = in_ref[...].astype(jnp.float32).reshape(8, 4, N_IN, WIDTH)
    parts = []
    for q in range(4):
        x = data[:, q].reshape(rows, WIDTH)
        parts.append([x[:, t * LANES : (t + 1) * LANES] for t in range(n_tiles)])
    for k in range(N_Y):
        tiles = [zero] * n_tiles
        for q in range(4):
            move_lanes(parts[q], k * PIECE, PIECE, q * PIECE, tiles, lanes)
        for t in range(n_tiles):
            value = tiles[t].astype(jnp.bfloat16)
            out_ref[k * rows : (k + 1) * rows, t * LANES : (t + 1) * LANES] = value
            out_ref[(N_Y + k) * rows : (N_Y + k + 1) * rows, t * LANES : (t + 1) * LANES] = value


def unpack_kernel(in_ref, out_ref):
    rows = 64
    lanes = lane_ids(rows)
    n_tiles = WIDTH // LANES
    zero = jnp.zeros((rows, LANES), jnp.float32)
    for q in range(4):
        for p in range(2):
            cols = []
            for k in range(N_Y):
                tiles = [zero]
                for h in range(2):
                    base = (h * N_Y + k) * rows
                    start = q * PIECE + p * N_FR
                    need = range(start // LANES, (start + N_FR - 1) // LANES + 1)
                    src = {
                        t: in_ref[base : base + rows, t * LANES : (t + 1) * LANES].astype(jnp.float32)
                        for t in need
                    }
                    move_lanes(src, start, N_FR, h * N_FR, tiles, lanes)
                cols.append(tiles[0].reshape(8, N_IN, LANES))
            value = jnp.concatenate(cols, axis=1)
            out_ref[:, q, :, p * LANES : (p + 1) * LANES] = value.astype(jnp.bfloat16)


def correlate_kernel(scale, row_ref, all_ref, out_ref):
    rows = out_ref.shape[2]
    cols = out_ref.shape[3]
    own = pl.multiple_of(row_ref[0], rows)
    col = pl.multiple_of(pl.program_id(0) * cols, cols)
    a0 = all_ref[0, pl.ds(own, rows), :]
    a1 = all_ref[1, pl.ds(own, rows), :]
    b = jnp.concatenate([all_ref[0, pl.ds(col, cols), :], all_ref[1, pl.ds(col, cols), :]], axis=1)
    plain = jnp.concatenate([a0, a1], axis=1)
    crossed = jnp.concatenate([a0[:, LANES:], -a0[:, :LANES], a1[:, LANES:], -a1[:, :LANES]], axis=1)
    out_ref[0, 0] = dot_t(plain, b) * scale
    out_ref[1, 0] = dot_t(crossed, b) * scale


def per_device(voltages, fir_taps):
    in_dev, length = voltages.shape
    margin = (TAPS - 1) * FRAME
    tail = voltages[:, length - margin :]
    halo = lax.ppermute(tail, ("yhi", "core"), [(i, i + 1) for i in range(N_TB - 1)])
    high, low = dft_tables()
    spectra = pl.pallas_call(
        channelize_kernel,
        out_shape=jax.ShapeDtypeStruct((N_ZX * N_IN, WIDTH), jnp.bfloat16),
        in_specs=[VMEM] * 5,
        out_specs=VMEM,
        scratch_shapes=[
            pltpu.VMEM((FRAME // LANES, N_FR * N_IN, LANES), jnp.float32),
            pltpu.VMEM((64 * N_IN, FRAME), jnp.bfloat16),
            pltpu.VMEM((64 * N_IN, FRAME), jnp.bfloat16),
            pltpu.VMEM((WIDTH // LANES, N_ZX * N_IN, LANES), jnp.float32),
        ],
        compiler_params=PARAMS,
        name="channelize",
    )(halo, voltages, fir_taps, jnp.asarray(high), jnp.asarray(low))
    first = lax.all_to_all(spectra.reshape(N_ZX, N_IN, WIDTH), ("z", "x"), 0, 0, tiled=True)
    packed = pl.pallas_call(
        repack_kernel,
        out_shape=jax.ShapeDtypeStruct((2 * N_Y * 64, WIDTH), jnp.bfloat16),
        in_specs=[VMEM],
        out_specs=VMEM,
        compiler_params=PARAMS,
        name="repack",
    )(first.reshape(N_ZX * N_IN, WIDTH))
    second = lax.all_to_all(packed.reshape(2 * N_Y, 64, WIDTH), ("yhi", "ylo"), 0, 0, tiled=True)
    half = pl.pallas_call(
        unpack_kernel,
        out_shape=jax.ShapeDtypeStruct((8, 4, N_Y * N_IN, 2 * LANES), jnp.bfloat16),
        in_specs=[VMEM],
        out_specs=VMEM,
        compiler_params=PARAMS,
        name="unpack",
    )(second.reshape(2 * N_Y * 64, WIDTH))
    n_inputs = N_ZX * N_Y * N_IN
    whole = lax.all_gather(half.reshape(n_inputs, 2 * LANES), "core", axis=0, tiled=False)
    rows = n_inputs // N_TB
    cols = 256
    row_start = ((lax.axis_index("yhi") * 2 + lax.axis_index("core")) * rows).astype(jnp.int32).reshape(1)
    scale = np.float32(1.0 / (N_FR * N_TB))
    return pl.pallas_call(
        lambda *refs: correlate_kernel(scale, *refs),
        grid=(n_inputs // cols,),
        out_shape=jax.ShapeDtypeStruct((2, 1, rows, n_inputs), jnp.float32),
        in_specs=[pl.BlockSpec(memory_space=pltpu.SMEM), VMEM],
        out_specs=pl.BlockSpec((2, 1, rows, cols), lambda j: (0, 0, 0, j)),
        compiler_params=PARAMS,
        name="correlate",
    )(row_start, whole)


def solution(mesh):
    fine = Mesh(mesh.devices.reshape(8, 4, 4, 2, 2), ("z", "x", "ylo", "yhi", "core"))
    in_specs = (P(("z", "x", "ylo"), ("yhi", "core")), P())
    out_specs = P(None, ("z", "x", "ylo"), ("yhi", "core"), None)
    return jax.shard_map(
        per_device, mesh=fine, in_specs=in_specs, out_specs=out_specs, check_vma=False
    )
```

```python
import math

import jax
import jax.numpy as jnp
import numpy as np
from jax import lax
from jax.experimental import pallas as pl
from jax.experimental.pallas import tpu as pltpu
from jax.sharding import Mesh
from jax.sharding import PartitionSpec as P

CH = 128
OFFSET = 64
FRAME = 512
TAPS = 12
MARGIN = TAPS - 1
N_IN = 8
N_FR = 48
N_TB = 4
SLOTS = N_FR + MARGIN
HALF = 64
LANES = 128
N_INPUTS = 1024
SWAP = [(0, 1), (1, 0)]
VMEM = pl.BlockSpec(memory_space=pltpu.VMEM)
SMEM = pl.BlockSpec(memory_space=pltpu.SMEM)
PARAMS = pltpu.CompilerParams(vmem_limit_bytes=40 * 1024 * 1024)

LOW_SLOT = N_FR - MARGIN
HIGH_SLOT = N_FR


def dft_tables():
    phase = (np.arange(CH)[:, None] + OFFSET) * np.arange(FRAME)[None, :] % FRAME
    angle = phase * (2.0 * math.pi / FRAME)
    table = np.concatenate([np.cos(angle), -np.sin(angle)], 0) / math.sqrt(FRAME)
    high = table.astype(jnp.bfloat16)
    low = (table - high.astype(np.float64)).astype(jnp.bfloat16)
    return high, low


def dot_t(a, b):
    return lax.dot_general(a, b, (((1,), (1,)), ((), ())), preferred_element_type=jnp.float32)


def lane_ids(rows):
    return lax.broadcasted_iota(jnp.int32, (rows, LANES), 1)


def channelize_kernel(
    place_ref, volt_ref, other_ref, taps_ref, high_ref, low_ref, out_ref, frames, filt, fhigh, flow, spread
):
    core, yhi = place_ref[0], place_ref[1]
    edge = MARGIN * FRAME
    own = N_FR * FRAME
    nothing = jnp.zeros((N_IN, edge), jnp.bfloat16)

    @pl.when(core == 0)
    def _():
        frames[:, :edge] = nothing
        frames[:, edge : edge + own] = volt_ref[...]
        frames[:, edge + own :] = other_ref[:, :edge]

    @pl.when(core == 1)
    def _():
        frames[:, :own] = volt_ref[...]

    @pl.when((core == 1) & (yhi == 0))
    def _():
        frames[:, own : own + edge] = volt_ref[:, own - edge :]
        frames[:, own + edge :] = nothing

    @pl.when((core == 1) & (yhi == 1))
    def _():
        frames[:, own : own + edge] = nothing
        frames[:, own + edge :] = other_ref[:, :edge]

    @pl.loop(0, FRAME // LANES)
    def _(block):
        lo = pl.multiple_of(block * LANES, LANES)
        taps = [jnp.broadcast_to(taps_ref[k : k + 1, pl.ds(lo, LANES)], (N_IN, LANES)) for k in range(TAPS)]
        window = []
        for t in range(SLOTS + MARGIN):
            window.append(frames[:, pl.ds(pl.multiple_of(t * FRAME + lo, LANES), LANES)].astype(jnp.float32))
            if t < MARGIN:
                continue
            total = taps[0] * window[0]
            for k in range(1, TAPS):
                total = total + taps[k] * window[k]
            window.pop(0)
            f = t - MARGIN
            filt[block, f * N_IN : (f + 1) * N_IN, :] = total
        filt[block, SLOTS * N_IN :, :] = jnp.zeros(((HALF - SLOTS) * N_IN, LANES), jnp.float32)

    for i in range(N_IN):
        for block in range(FRAME // LANES):
            x = filt[block, pl.ds(i, HALF, stride=N_IN), :]
            high = x.astype(jnp.bfloat16)
            low = (x - high.astype(jnp.float32)).astype(jnp.bfloat16)
            fhigh[i * HALF : (i + 1) * HALF, block * LANES : (block + 1) * LANES] = high
            flow[i * HALF : (i + 1) * HALF, block * LANES : (block + 1) * LANES] = low

    lanes = lane_ids(CH)
    slot = lanes % HALF
    drop = (slot < MARGIN) & (core == 0) & (yhi == 1)
    split = (slot >= LOW_SLOT) & (slot < HIGH_SLOT) & (core == 1)
    for pair in range(N_IN // 2):
        fh = fhigh[pair * LANES : (pair + 1) * LANES, :]
        fl = flow[pair * LANES : (pair + 1) * LANES, :]
        spec = dot_t(high_ref[...], fh) + (dot_t(high_ref[...], fl) + dot_t(low_ref[...], fh))
        real, imag = spec[:CH], spec[CH:]
        first = jnp.where(lanes < HALF, real, pltpu.roll(imag, HALF, 1))
        second = jnp.where(lanes < HALF, pltpu.roll(real, HALF, 1), imag)
        for sub, value in enumerate((first, second)):
            rest = value - value.astype(jnp.bfloat16).astype(jnp.float32)
            value = jnp.where(split, pltpu.roll(rest, LANES - MARGIN, 1), value)
            value = jnp.where(drop, 0.0, value)
            spread[pl.ds(pair * 2 + sub, CH, stride=N_IN), :] = value
    out_ref[...] = spread[...].astype(jnp.bfloat16)


def correlate_kernel(scale, place_ref, own_ref, far_ref, near_ref, cross_ref, out_ref, cols_ref, rows_ref):
    core, yhi = place_ref[0], place_ref[1]
    rows = out_ref.shape[2]
    cols = out_ref.shape[3]

    def lay(plain, parts):
        cols_ref[:, :LANES] = plain[0][...]
        cols_ref[:, LANES : 2 * LANES] = plain[1][...]
        slot = lane_ids(N_INPUTS) % HALF
        edge = (slot >= HIGH_SLOT) & (slot < SLOTS)
        low = (slot >= LOW_SLOT) & (slot < HIGH_SLOT)
        a, b = parts[0][...].astype(jnp.float32), parts[1][...].astype(jnp.float32)
        total = (a + pltpu.roll(a, MARGIN, 1)) + (b + pltpu.roll(b, MARGIN, 1))
        one = jnp.where(edge, total, jnp.where(low, 0.0, a))
        two = jnp.where(edge | low, 0.0, b)
        cols_ref[:, 2 * LANES : 3 * LANES] = one.astype(jnp.bfloat16)
        cols_ref[:, 3 * LANES :] = two.astype(jnp.bfloat16)

    @pl.when(pl.program_id(0) == 0)
    def _():
        @pl.when(core == 0)
        def _():
            lay((own_ref, far_ref), (near_ref, cross_ref))

        @pl.when(core == 1)
        def _():
            lay((near_ref, cross_ref), (own_ref, far_ref))

        own = pl.multiple_of((yhi * 2 + core) * rows, rows)
        lanes = lane_ids(rows)
        for t in range(N_TB):
            x = cols_ref[pl.ds(own, rows), t * LANES : (t + 1) * LANES]
            rows_ref[0, :, t * LANES : (t + 1) * LANES] = x
            turned = pltpu.roll(x.astype(jnp.float32), HALF, 1)
            turned = jnp.where(lanes < HALF, turned, -turned)
            rows_ref[1, :, t * LANES : (t + 1) * LANES] = turned.astype(jnp.bfloat16)

    col = pl.multiple_of(pl.program_id(0) * cols, cols)
    b = cols_ref[pl.ds(col, cols), :]
    out_ref[0, 0] = dot_t(rows_ref[0], b) * scale
    out_ref[1, 0] = dot_t(rows_ref[1], b) * scale


def per_device(voltages, fir_taps):
    place = jnp.stack([lax.axis_index("core"), lax.axis_index("yhi")]).astype(jnp.int32)
    other = lax.ppermute(voltages, "core", SWAP)
    high, low = dft_tables()
    spectra = pl.pallas_call(
        channelize_kernel,
        out_shape=jax.ShapeDtypeStruct((CH * N_IN, LANES), jnp.bfloat16),
        in_specs=[SMEM] + [VMEM] * 5,
        out_specs=VMEM,
        scratch_shapes=[
            pltpu.VMEM((N_IN, (SLOTS + MARGIN) * FRAME), jnp.bfloat16),
            pltpu.VMEM((FRAME // LANES, HALF * N_IN, LANES), jnp.float32),
            pltpu.VMEM((HALF * N_IN, FRAME), jnp.bfloat16),
            pltpu.VMEM((HALF * N_IN, FRAME), jnp.bfloat16),
            pltpu.VMEM((CH * N_IN, LANES), jnp.float32),
        ],
        compiler_params=PARAMS,
        name="channelize",
    )(place, voltages, other, fir_taps, jnp.asarray(high), jnp.asarray(low))
    turned = lax.all_to_all(spectra.reshape(CH, N_IN, LANES), ("z", "x", "ylo"), 0, 0, tiled=True)
    own = turned.reshape(N_INPUTS, LANES)
    far = lax.ppermute(own, "yhi", SWAP)
    near = lax.ppermute(own, "core", SWAP)
    cross = lax.ppermute(far, "core", SWAP)
    rows = N_INPUTS // N_TB
    cols = 256
    scale = np.float32(1.0 / (N_FR * N_TB))
    return pl.pallas_call(
        lambda *refs: correlate_kernel(scale, *refs),
        grid=(N_INPUTS // cols,),
        out_shape=jax.ShapeDtypeStruct((2, 1, rows, N_INPUTS), jnp.float32),
        in_specs=[SMEM] + [VMEM] * 4,
        out_specs=pl.BlockSpec((2, 1, rows, cols), lambda j: (0, 0, 0, j)),
        scratch_shapes=[
            pltpu.VMEM((N_INPUTS, N_TB * LANES), jnp.bfloat16),
            pltpu.VMEM((2, rows, N_TB * LANES), jnp.bfloat16),
        ],
        compiler_params=PARAMS,
        name="correlate",
    )(place, own, far, near, cross)


def solution(mesh):
    fine = Mesh(mesh.devices.reshape(8, 4, 4, 2, 2), ("z", "x", "ylo", "yhi", "core"))
    in_specs = (P(("z", "x", "ylo"), ("yhi", "core")), P())
    out_specs = P(None, ("z", "x", "ylo"), ("yhi", "core"), None)
    return jax.shard_map(
        per_device, mesh=fine, in_specs=in_specs, out_specs=out_specs, check_vma=False
    )
```

```python
import math

import jax
import jax.numpy as jnp
import numpy as np
from jax import lax
from jax.experimental import pallas as pl
from jax.experimental.pallas import tpu as pltpu
from jax.sharding import Mesh
from jax.sharding import PartitionSpec as P

CH = 128
OFFSET = 64
FRAME = 512
TAPS = 12
MARGIN = TAPS - 1
N_IN = 8
N_FR = 48
N_TB = 4
SLOTS = N_FR + MARGIN
HALF = 64
LANES = 128
N_INPUTS = 1024
SWAP = [(0, 1), (1, 0)]
HBM = pl.BlockSpec(memory_space=pltpu.HBM)
VMEM = pl.BlockSpec(memory_space=pltpu.VMEM)
PARAMS = pltpu.CompilerParams(vmem_limit_bytes=40 * 1024 * 1024)

LOW_SLOT = N_FR - MARGIN
HIGH_SLOT = N_FR
SPARE = HALF - SLOTS
RIDERS = -(-SLOTS // SPARE)


def dft_tables():
    phase = (np.arange(CH)[:, None] + OFFSET) * np.arange(FRAME)[None, :] % FRAME
    angle = phase * (2.0 * math.pi / FRAME)
    table = np.concatenate([np.cos(angle), -np.sin(angle)], 0) / math.sqrt(FRAME)
    high = table.astype(jnp.bfloat16)
    low = (table - high.astype(np.float64)).astype(jnp.bfloat16)
    return high, low


def dot_t(a, b):
    return lax.dot_general(a, b, (((1,), (1,)), ((), ())), preferred_element_type=jnp.float32)


def lane_ids(rows):
    return lax.broadcasted_iota(jnp.int32, (rows, LANES), 1)


def fetch(pairs, sems):
    copies = [pltpu.make_async_copy(src, dst, sems.at[n]) for n, (src, dst) in enumerate(pairs)]
    for copy in copies:
        copy.start()
    return copies


def run_filter(taps_ref, frame_at, keep, count, block):
    lo = pl.multiple_of(block * LANES, LANES)
    taps = [jnp.broadcast_to(taps_ref[k : k + 1, pl.ds(lo, LANES)], (N_IN, LANES)) for k in range(TAPS)]
    window = []
    for t in range(count + MARGIN):
        window.append(frame_at(t, lo).astype(jnp.float32))
        if t < MARGIN:
            continue
        total = taps[0] * window[0]
        for k in range(1, TAPS):
            total = total + taps[k] * window[k]
        window.pop(0)
        keep(t - MARGIN, total)


def pieces(x):
    high = x.astype(jnp.bfloat16)
    return high, (x - high.astype(jnp.float32)).astype(jnp.bfloat16)


def at(t, lo):
    return pl.ds(pl.multiple_of(t * FRAME + lo, LANES), LANES)


def prefilter_kernel(
    volt_hbm, taps_hbm, high_hbm, low_hbm, fhigh, flow, seam, taps_ref, high_ref, low_ref, frames, filt, sems
):
    core, yhi = lax.axis_index("core"), lax.axis_index("yhi")
    edge = MARGIN * FRAME
    own = N_FR * FRAME
    nothing = jnp.zeros((N_IN, edge), jnp.bfloat16)
    offset = pl.multiple_of((1 - core) * edge, LANES)
    copies = fetch(
        [
            (volt_hbm, frames.at[:, pl.ds(offset, own)]),
            (taps_hbm, taps_ref),
            (high_hbm, high_ref),
            (low_hbm, low_ref),
        ],
        sems,
    )
    tail = pltpu.make_async_copy(volt_hbm.at[:, pl.ds(own - edge, edge)], frames.at[:, pl.ds(own, edge)], sems.at[4])
    second = (core == 1) & (yhi == 0)

    @pl.when(second)
    def _():
        tail.start()

    @pl.when(core == 0)
    def _():
        frames[:, :edge] = nothing

    @pl.when((core == 1) & (yhi == 1))
    def _():
        frames[:, own:] = nothing

    copies[0].wait()
    copies[1].wait()

    @pl.when(second)
    def _():
        tail.wait()

    seam[...] = frames[:, own:]

    @pl.loop(0, FRAME // LANES)
    def _(block):
        def keep(f, x):
            filt[block, f * N_IN : (f + 1) * N_IN, :] = x

        run_filter(taps_ref, lambda t, lo: frames[:, at(t, lo)], keep, N_FR, block)

    for i in range(N_IN):
        for block in range(FRAME // LANES):
            high, low = pieces(filt[block, pl.ds(i, N_FR, stride=N_IN), :])
            fhigh[i * N_FR : (i + 1) * N_FR, block * LANES : (block + 1) * LANES] = high
            flow[i * N_FR : (i + 1) * N_FR, block * LANES : (block + 1) * LANES] = low
    copies[2].wait()
    copies[3].wait()


def channelize_kernel(fhigh, flow, seam, other_ref, taps_ref, high_ref, low_ref, out_ref, filt, ghigh, glow, spread):
    core, yhi = lax.axis_index("core"), lax.axis_index("yhi")
    more = HALF - N_FR
    real_samples = (core == 0) | (yhi == 1)

    def frame_at(t, lo):
        if t < MARGIN:
            return seam[:, at(t, lo)]
        return jnp.where(real_samples, other_ref[:, at(t - MARGIN, lo)].astype(jnp.float32), 0.0)

    @pl.loop(0, FRAME // LANES)
    def _(block):
        def keep(f, x):
            filt[block, f * N_IN : (f + 1) * N_IN, :] = x

        run_filter(taps_ref, frame_at, keep, MARGIN, block)
        filt[block, MARGIN * N_IN :, :] = jnp.zeros(((more - MARGIN) * N_IN, LANES), jnp.float32)

    for i in range(N_IN):
        for block in range(FRAME // LANES):
            high, low = pieces(filt[block, pl.ds(i, more, stride=N_IN), :])
            ghigh[i * more : (i + 1) * more, block * LANES : (block + 1) * LANES] = high
            glow[i * more : (i + 1) * more, block * LANES : (block + 1) * LANES] = low

    lanes = lane_ids(CH)
    slot = lanes % HALF
    drop = (slot < MARGIN) & (core == 0) & (yhi == 1)
    split = (slot >= LOW_SLOT) & (slot < HIGH_SLOT) & (core == 1)

    def rows_of(f, g, i):
        return [f[i * N_FR : (i + 1) * N_FR, :], g[i * more : (i + 1) * more, :]]

    for pair in range(N_IN // 2):
        i = pair * 2
        fh = jnp.concatenate(rows_of(fhigh, ghigh, i) + rows_of(fhigh, ghigh, i + 1), 0)
        fl = jnp.concatenate(rows_of(flow, glow, i) + rows_of(flow, glow, i + 1), 0)
        spec = dot_t(high_ref[...], fh) + (dot_t(high_ref[...], fl) + dot_t(low_ref[...], fh))
        real, imag = spec[:CH], spec[CH:]
        first = jnp.where(lanes < HALF, real, pltpu.roll(imag, HALF, 1))
        second = jnp.where(lanes < HALF, pltpu.roll(real, HALF, 1), imag)
        for sub, value in enumerate((first, second)):
            rest = value - value.astype(jnp.bfloat16).astype(jnp.float32)
            value = jnp.where(split, pltpu.roll(rest, LANES - MARGIN, 1), value)
            value = jnp.where(drop, 0.0, value)
            spread[pl.ds(i + sub, CH, stride=N_IN), :] = value
    out_ref[...] = spread[...].astype(jnp.bfloat16)


def spare(lanes):
    return lanes % HALF >= SLOTS


def pack_kernel(in_ref, out_ref):
    lanes = lane_ids(N_IN)
    kept = out_ref.shape[0]
    last = in_ref[kept:, :].astype(jnp.float32)
    tiles = []
    for m in range(RIDERS):
        tile = in_ref[m * N_IN : (m + 1) * N_IN, :].astype(jnp.float32)
        tiles.append(jnp.where(spare(lanes), pltpu.roll(last, SLOTS - SPARE * m, 1), tile))
    out_ref[: RIDERS * N_IN, :] = jnp.concatenate(tiles, 0).astype(jnp.bfloat16)
    out_ref[RIDERS * N_IN :, :] = in_ref[RIDERS * N_IN : kept, :]


def unpack(ref, block):
    lanes = lane_ids(N_IN)
    slot = lanes % HALF
    carriers = ref[block, : RIDERS * N_IN, :].astype(jnp.float32)
    last = jnp.zeros((N_IN, LANES), jnp.float32)
    tiles = []
    for m in range(RIDERS):
        tile = carriers[m * N_IN : (m + 1) * N_IN]
        moved = pltpu.roll(tile, (SPARE * m - SLOTS) % LANES, 1)
        last = jnp.where((slot >= SPARE * m) & (slot < SPARE * (m + 1)), moved, last)
        tiles.append(jnp.where(spare(lanes), 0.0, tile))
    last = jnp.where(spare(lanes), 0.0, last)
    rest = ref[block, RIDERS * N_IN :, :].astype(jnp.float32)
    return jnp.concatenate(tiles + [rest, last], 0)


def correlate_kernel(scale, all_ref, out_hbm, cols_ref, rows_ref, out_ref, sems):
    core, yhi = lax.axis_index("core"), lax.axis_index("yhi")
    chunks, _, rows, cols = out_ref.shape
    cols_ref[:, :LANES] = unpack(all_ref, 0).astype(jnp.bfloat16)
    cols_ref[:, LANES : 2 * LANES] = unpack(all_ref, 2).astype(jnp.bfloat16)
    slot = lane_ids(N_INPUTS) % HALF
    edge = (slot >= HIGH_SLOT) & (slot < SLOTS)
    low = (slot >= LOW_SLOT) & (slot < HIGH_SLOT)
    a, b = unpack(all_ref, 1), unpack(all_ref, 3)
    total = (a + pltpu.roll(a, MARGIN, 1)) + (b + pltpu.roll(b, MARGIN, 1))
    one = jnp.where(edge, total, jnp.where(low, 0.0, a))
    two = jnp.where(edge | low, 0.0, b)
    cols_ref[:, 2 * LANES : 3 * LANES] = one.astype(jnp.bfloat16)
    cols_ref[:, 3 * LANES :] = two.astype(jnp.bfloat16)

    own = pl.multiple_of((yhi * 2 + core) * rows, rows)
    lanes = lane_ids(rows)
    for t in range(N_TB):
        x = cols_ref[pl.ds(own, rows), t * LANES : (t + 1) * LANES]
        rows_ref[0, :, t * LANES : (t + 1) * LANES] = x
        turned = pltpu.roll(x.astype(jnp.float32), HALF, 1)
        turned = jnp.where(lanes < HALF, turned, -turned)
        rows_ref[1, :, t * LANES : (t + 1) * LANES] = turned.astype(jnp.bfloat16)

    copies = []
    for j in range(chunks):
        cut = slice(j * cols, (j + 1) * cols)
        for part in range(2):
            out_ref[j, part] = dot_t(rows_ref[part], cols_ref[cut, :]) * scale
            copy = pltpu.make_async_copy(out_ref.at[j, part], out_hbm.at[part, 0, :, cut], sems.at[j, part])
            copy.start()
            copies.append(copy)
    for copy in copies:
        copy.wait()


def far_memory(x):
    return pltpu.with_memory_space_constraint(x, pltpu.HBM)


def per_device(voltages, fir_taps):
    other = lax.ppermute(voltages, "core", SWAP)
    high, low = (jnp.asarray(table) for table in dft_tables())
    seam_shape = (N_IN, MARGIN * FRAME)
    fhigh, flow, seam, taps, high, low = pl.pallas_call(
        prefilter_kernel,
        out_shape=[
            jax.ShapeDtypeStruct((N_IN * N_FR, FRAME), jnp.bfloat16),
            jax.ShapeDtypeStruct((N_IN * N_FR, FRAME), jnp.bfloat16),
            jax.ShapeDtypeStruct(seam_shape, jnp.bfloat16),
            jax.ShapeDtypeStruct(fir_taps.shape, jnp.float32),
            jax.ShapeDtypeStruct(high.shape, jnp.bfloat16),
            jax.ShapeDtypeStruct(low.shape, jnp.bfloat16),
        ],
        in_specs=[HBM] * 4,
        out_specs=[VMEM] * 6,
        scratch_shapes=[
            pltpu.VMEM((N_IN, SLOTS * FRAME), jnp.bfloat16),
            pltpu.VMEM((FRAME // LANES, N_FR * N_IN, LANES), jnp.float32),
            pltpu.SemaphoreType.DMA((5,)),
        ],
        compiler_params=PARAMS,
        cost_estimate=pl.CostEstimate(flops=10**8, bytes_accessed=4 * 10**6, transcendentals=0),
        name="prefilter",
    )(*(far_memory(x) for x in (voltages, fir_taps, high, low)))
    more = HALF - N_FR
    spectra = pl.pallas_call(
        channelize_kernel,
        out_shape=jax.ShapeDtypeStruct((CH * N_IN, LANES), jnp.bfloat16),
        in_specs=[VMEM] * 7,
        out_specs=VMEM,
        scratch_shapes=[
            pltpu.VMEM((FRAME // LANES, more * N_IN, LANES), jnp.float32),
            pltpu.VMEM((more * N_IN, FRAME), jnp.bfloat16),
            pltpu.VMEM((more * N_IN, FRAME), jnp.bfloat16),
            pltpu.VMEM((CH * N_IN, LANES), jnp.float32),
        ],
        compiler_params=PARAMS,
        name="channelize",
    )(fhigh, flow, seam, other, taps, high, low)
    turned = lax.all_to_all(spectra.reshape(CH, N_IN, LANES), ("z", "x", "ylo"), 0, 0, tiled=True)
    packed = pl.pallas_call(
        pack_kernel,
        out_shape=jax.ShapeDtypeStruct((N_INPUTS - N_IN, LANES), jnp.bfloat16),
        in_specs=[VMEM],
        out_specs=VMEM,
        compiler_params=PARAMS,
        name="pack",
    )(turned.reshape(N_INPUTS, LANES))
    blocks = lax.all_gather(packed, ("yhi", "core"), axis=0, tiled=False)
    rows = N_INPUTS // N_TB
    cols = 256
    scale = np.float32(1.0 / (N_FR * N_TB))
    return pl.pallas_call(
        lambda *refs: correlate_kernel(scale, *refs),
        out_shape=jax.ShapeDtypeStruct((2, 1, rows, N_INPUTS), jnp.float32),
        in_specs=[VMEM],
        out_specs=HBM,
        scratch_shapes=[
            pltpu.VMEM((N_INPUTS, N_TB * LANES), jnp.bfloat16),
            pltpu.VMEM((2, rows, N_TB * LANES), jnp.bfloat16),
            pltpu.VMEM((N_INPUTS // cols, 2, rows, cols), jnp.float32),
            pltpu.SemaphoreType.DMA((N_INPUTS // cols, 2)),
        ],
        compiler_params=PARAMS,
        name="correlate",
    )(blocks)


def solution(mesh):
    fine = Mesh(mesh.devices.reshape(8, 4, 4, 2, 2), ("z", "x", "ylo", "yhi", "core"))
    in_specs = (P(("z", "x", "ylo"), ("yhi", "core")), P())
    out_specs = P(None, ("z", "x", "ylo"), ("yhi", "core"), None)
    return jax.shard_map(
        per_device, mesh=fine, in_specs=in_specs, out_specs=out_specs, check_vma=False
    )
```

```python
import math

import jax
import jax.numpy as jnp
import numpy as np
from jax import lax
from jax.experimental import pallas as pl
from jax.experimental.pallas import tpu as pltpu
from jax.sharding import Mesh
from jax.sharding import PartitionSpec as P

CH = 128
OFFSET = 64
FRAME = 512
TAPS = 12
MARGIN = TAPS - 1
N_IN = 8
N_FR = 48
N_TB = 4
SLOTS = N_FR + MARGIN
HALF = 64
LANES = 128
N_INPUTS = 1024
SWAP = [(0, 1), (1, 0)]
HBM = pl.BlockSpec(memory_space=pltpu.HBM)
VMEM = pl.BlockSpec(memory_space=pltpu.VMEM)
PARAMS = pltpu.CompilerParams(vmem_limit_bytes=40 * 1024 * 1024)

LOW_SLOT = N_FR - MARGIN
HIGH_SLOT = N_FR


def dft_tables():
    phase = (np.arange(CH)[:, None] + OFFSET) * np.arange(FRAME)[None, :] % FRAME
    angle = phase * (2.0 * math.pi / FRAME)
    table = np.concatenate([np.cos(angle), -np.sin(angle)], 0) / math.sqrt(FRAME)
    high = table.astype(jnp.bfloat16)
    low = (table - high.astype(np.float64)).astype(jnp.bfloat16)
    return high, low


def dot_t(a, b):
    return lax.dot_general(a, b, (((1,), (1,)), ((), ())), preferred_element_type=jnp.float32)


def lane_ids(rows):
    return lax.broadcasted_iota(jnp.int32, (rows, LANES), 1)


def fetch(pairs, sems):
    copies = [pltpu.make_async_copy(src, dst, sems.at[n]) for n, (src, dst) in enumerate(pairs)]
    for copy in copies:
        copy.start()
    return copies


def run_filter(taps_ref, frame_at, keep, count, block):
    lo = pl.multiple_of(block * LANES, LANES)
    taps = [jnp.broadcast_to(taps_ref[k : k + 1, pl.ds(lo, LANES)], (N_IN, LANES)) for k in range(TAPS)]
    window = []
    for t in range(count + MARGIN):
        window.append(frame_at(t, lo).astype(jnp.float32))
        if t < MARGIN:
            continue
        total = taps[0] * window[0]
        for k in range(1, TAPS):
            total = total + taps[k] * window[k]
        window.pop(0)
        keep(t - MARGIN, total)


def pieces(x):
    high = x.astype(jnp.bfloat16)
    return high, (x - high.astype(jnp.float32)).astype(jnp.bfloat16)


def at(t, lo):
    return pl.ds(pl.multiple_of(t * FRAME + lo, LANES), LANES)


def prefilter_kernel(
    volt_hbm, taps_hbm, high_hbm, low_hbm, fhigh, flow, seam, taps_ref, high_ref, low_ref, frames, filt, sems
):
    core, yhi = lax.axis_index("core"), lax.axis_index("yhi")
    edge = MARGIN * FRAME
    own = N_FR * FRAME
    nothing = jnp.zeros((N_IN, edge), jnp.bfloat16)
    offset = pl.multiple_of((1 - core) * edge, LANES)
    copies = fetch(
        [
            (volt_hbm, frames.at[:, pl.ds(offset, own)]),
            (taps_hbm, taps_ref),
            (high_hbm, high_ref),
            (low_hbm, low_ref),
        ],
        sems,
    )
    tail = pltpu.make_async_copy(volt_hbm.at[:, pl.ds(own - edge, edge)], frames.at[:, pl.ds(own, edge)], sems.at[4])
    second = (core == 1) & (yhi == 0)

    @pl.when(second)
    def _():
        tail.start()

    @pl.when(core == 0)
    def _():
        frames[:, :edge] = nothing

    @pl.when((core == 1) & (yhi == 1))
    def _():
        frames[:, own:] = nothing

    copies[0].wait()
    copies[1].wait()

    @pl.when(second)
    def _():
        tail.wait()

    seam[...] = frames[:, own:]

    @pl.loop(0, FRAME // LANES)
    def _(block):
        def keep(f, x):
            filt[block, f * N_IN : (f + 1) * N_IN, :] = x

        run_filter(taps_ref, lambda t, lo: frames[:, at(t, lo)], keep, N_FR, block)

    for i in range(N_IN):
        for block in range(FRAME // LANES):
            high, low = pieces(filt[block, pl.ds(i, N_FR, stride=N_IN), :])
            fhigh[i * N_FR : (i + 1) * N_FR, block * LANES : (block + 1) * LANES] = high
            flow[i * N_FR : (i + 1) * N_FR, block * LANES : (block + 1) * LANES] = low
    copies[2].wait()
    copies[3].wait()


def channelize_kernel(fhigh, flow, seam, other_ref, taps_ref, high_ref, low_ref, out_ref, filt, ghigh, glow, spread):
    core, yhi = lax.axis_index("core"), lax.axis_index("yhi")
    more = HALF - N_FR
    real_samples = (core == 0) | (yhi == 1)

    def frame_at(t, lo):
        if t < MARGIN:
            return seam[:, at(t, lo)]
        return jnp.where(real_samples, other_ref[:, at(t - MARGIN, lo)].astype(jnp.float32), 0.0)

    @pl.loop(0, FRAME // LANES)
    def _(block):
        def keep(f, x):
            filt[block, f * N_IN : (f + 1) * N_IN, :] = x

        run_filter(taps_ref, frame_at, keep, MARGIN, block)
        filt[block, MARGIN * N_IN :, :] = jnp.zeros(((more - MARGIN) * N_IN, LANES), jnp.float32)

    for i in range(N_IN):
        for block in range(FRAME // LANES):
            high, low = pieces(filt[block, pl.ds(i, more, stride=N_IN), :])
            ghigh[i * more : (i + 1) * more, block * LANES : (block + 1) * LANES] = high
            glow[i * more : (i + 1) * more, block * LANES : (block + 1) * LANES] = low

    lanes = lane_ids(CH)
    slot = lanes % HALF
    drop = (slot < MARGIN) & (core == 0) & (yhi == 1)
    split = (slot >= LOW_SLOT) & (slot < HIGH_SLOT) & (core == 1)

    def rows_of(f, g, i):
        return [f[i * N_FR : (i + 1) * N_FR, :], g[i * more : (i + 1) * more, :]]

    for pair in range(N_IN // 2):
        i = pair * 2
        fh = jnp.concatenate(rows_of(fhigh, ghigh, i) + rows_of(fhigh, ghigh, i + 1), 0)
        fl = jnp.concatenate(rows_of(flow, glow, i) + rows_of(flow, glow, i + 1), 0)
        spec = dot_t(high_ref[...], fh) + (dot_t(high_ref[...], fl) + dot_t(low_ref[...], fh))
        real, imag = spec[:CH], spec[CH:]
        first = jnp.where(lanes < HALF, real, pltpu.roll(imag, HALF, 1))
        second = jnp.where(lanes < HALF, pltpu.roll(real, HALF, 1), imag)
        for sub, value in enumerate((first, second)):
            rest = value - value.astype(jnp.bfloat16).astype(jnp.float32)
            value = jnp.where(split, pltpu.roll(rest, LANES - MARGIN, 1), value)
            value = jnp.where(drop, 0.0, value)
            spread[pl.ds(i + sub, CH, stride=N_IN), :] = value
    result = spread[...].astype(jnp.bfloat16)
    for copy in range(2):
        out_ref[copy * CH * N_IN : (copy + 1) * CH * N_IN, :] = result


def lay(in_ref, cols_ref, rows_ref, parts):
    core, yhi = lax.axis_index("core"), lax.axis_index("yhi")
    rows = rows_ref.shape[1]

    @pl.when(jnp.logical_not(parts))
    def _():
        for t in range(2):
            cols_ref[:, t * LANES : (t + 1) * LANES] = in_ref[t * N_INPUTS : (t + 1) * N_INPUTS, :]

    @pl.when(parts)
    def _():
        slot = lane_ids(N_INPUTS) % HALF
        edge = (slot >= HIGH_SLOT) & (slot < SLOTS)
        low = (slot >= LOW_SLOT) & (slot < HIGH_SLOT)
        a = in_ref[:N_INPUTS, :].astype(jnp.float32)
        b = in_ref[N_INPUTS:, :].astype(jnp.float32)
        total = (a + pltpu.roll(a, MARGIN, 1)) + (b + pltpu.roll(b, MARGIN, 1))
        one = jnp.where(edge, total, jnp.where(low, 0.0, a))
        two = jnp.where(edge | low, 0.0, b)
        cols_ref[:, :LANES] = one.astype(jnp.bfloat16)
        cols_ref[:, LANES:] = two.astype(jnp.bfloat16)

    own = pl.multiple_of((yhi * 2 + core) * rows, rows)
    lanes = lane_ids(rows)
    for t in range(2):
        x = cols_ref[pl.ds(own, rows), t * LANES : (t + 1) * LANES]
        rows_ref[0, :, t * LANES : (t + 1) * LANES] = x
        turned = pltpu.roll(x.astype(jnp.float32), HALF, 1)
        turned = jnp.where(lanes < HALF, turned, -turned)
        rows_ref[1, :, t * LANES : (t + 1) * LANES] = turned.astype(jnp.bfloat16)


def first_half_kernel(in_ref, part_ref, cols_ref, rows_ref):
    lay(in_ref, cols_ref, rows_ref, lax.axis_index("core") == 1)
    cols = part_ref.shape[3]
    for j in range(part_ref.shape[0]):
        for part in range(2):
            part_ref[j, part] = dot_t(rows_ref[part], cols_ref[j * cols : (j + 1) * cols, :])


def second_half_kernel(scale, in_ref, part_ref, out_hbm, cols_ref, rows_ref, out_ref, sems):
    lay(in_ref, cols_ref, rows_ref, lax.axis_index("core") == 0)
    chunks, _, _, cols = out_ref.shape
    copies = []
    for j in range(chunks):
        cut = slice(j * cols, (j + 1) * cols)
        for part in range(2):
            out_ref[j, part] = (part_ref[j, part] + dot_t(rows_ref[part], cols_ref[cut, :])) * scale
            copy = pltpu.make_async_copy(out_ref.at[j, part], out_hbm.at[part, 0, :, cut], sems.at[j, part])
            copy.start()
            copies.append(copy)
    for copy in copies:
        copy.wait()


def far_memory(x):
    return pltpu.with_memory_space_constraint(x, pltpu.HBM)


def per_device(voltages, fir_taps):
    other = lax.ppermute(voltages, "core", SWAP)
    high, low = (jnp.asarray(table) for table in dft_tables())
    seam_shape = (N_IN, MARGIN * FRAME)
    fhigh, flow, seam, taps, high, low = pl.pallas_call(
        prefilter_kernel,
        out_shape=[
            jax.ShapeDtypeStruct((N_IN * N_FR, FRAME), jnp.bfloat16),
            jax.ShapeDtypeStruct((N_IN * N_FR, FRAME), jnp.bfloat16),
            jax.ShapeDtypeStruct(seam_shape, jnp.bfloat16),
            jax.ShapeDtypeStruct(fir_taps.shape, jnp.float32),
            jax.ShapeDtypeStruct(high.shape, jnp.bfloat16),
            jax.ShapeDtypeStruct(low.shape, jnp.bfloat16),
        ],
        in_specs=[HBM] * 4,
        out_specs=[VMEM] * 6,
        scratch_shapes=[
            pltpu.VMEM((N_IN, SLOTS * FRAME), jnp.bfloat16),
            pltpu.VMEM((FRAME // LANES, N_FR * N_IN, LANES), jnp.float32),
            pltpu.SemaphoreType.DMA((5,)),
        ],
        compiler_params=PARAMS,
        cost_estimate=pl.CostEstimate(flops=10**8, bytes_accessed=4 * 10**6, transcendentals=0),
        name="prefilter",
    )(*(far_memory(x) for x in (voltages, fir_taps, high, low)))
    more = HALF - N_FR
    spectra = pl.pallas_call(
        channelize_kernel,
        out_shape=jax.ShapeDtypeStruct((2 * CH * N_IN, LANES), jnp.bfloat16),
        in_specs=[VMEM] * 7,
        out_specs=VMEM,
        scratch_shapes=[
            pltpu.VMEM((FRAME // LANES, more * N_IN, LANES), jnp.float32),
            pltpu.VMEM((more * N_IN, FRAME), jnp.bfloat16),
            pltpu.VMEM((more * N_IN, FRAME), jnp.bfloat16),
            pltpu.VMEM((CH * N_IN, LANES), jnp.float32),
        ],
        compiler_params=PARAMS,
        name="channelize",
    )(fhigh, flow, seam, other, taps, high, low)
    turned = lax.all_to_all(
        spectra.reshape(2 * CH, N_IN, LANES), ("yhi", "z", "x", "ylo"), 0, 0, tiled=True
    )
    own = turned.reshape(2 * N_INPUTS, LANES)
    other_core = lax.ppermute(own, "core", SWAP)
    rows = N_INPUTS // N_TB
    cols = 256
    chunks = N_INPUTS // cols
    operands = [
        pltpu.VMEM((N_INPUTS, 2 * LANES), jnp.bfloat16),
        pltpu.VMEM((2, rows, 2 * LANES), jnp.bfloat16),
    ]
    half = pl.pallas_call(
        first_half_kernel,
        out_shape=jax.ShapeDtypeStruct((chunks, 2, rows, cols), jnp.float32),
        in_specs=[VMEM],
        out_specs=VMEM,
        scratch_shapes=operands,
        compiler_params=PARAMS,
        cost_estimate=pl.CostEstimate(flops=3 * 10**8, bytes_accessed=3 * 10**6, transcendentals=0),
        name="first_half",
    )(own)
    scale = np.float32(1.0 / (N_FR * N_TB))
    return pl.pallas_call(
        lambda *refs: second_half_kernel(scale, *refs),
        out_shape=jax.ShapeDtypeStruct((2, 1, rows, N_INPUTS), jnp.float32),
        in_specs=[VMEM, VMEM],
        out_specs=HBM,
        scratch_shapes=operands
        + [
            pltpu.VMEM((chunks, 2, rows, cols), jnp.float32),
            pltpu.SemaphoreType.DMA((chunks, 2)),
        ],
        compiler_params=PARAMS,
        name="second_half",
    )(other_core, half)


def solution(mesh):
    fine = Mesh(mesh.devices.reshape(8, 4, 4, 2, 2), ("z", "x", "ylo", "yhi", "core"))
    in_specs = (P(("z", "x", "ylo"), ("yhi", "core")), P())
    out_specs = P(None, ("z", "x", "ylo"), ("yhi", "core"), None)
    return jax.shard_map(
        per_device, mesh=fine, in_specs=in_specs, out_specs=out_specs, check_vma=False
    )
```

```python
import math

import jax
import jax.numpy as jnp
import numpy as np
from jax import lax
from jax.experimental import pallas as pl
from jax.experimental.pallas import tpu as pltpu
from jax.sharding import Mesh
from jax.sharding import PartitionSpec as P

CH = 128
OFFSET = 64
FRAME = 512
TAPS = 12
MARGIN = TAPS - 1
N_IN = 8
N_FR = 48
N_TB = 4
N_Y = 4
SLOTS = N_FR + MARGIN
HALF = 64
LANES = 128
N_INPUTS = 1024
SWAP = [(0, 1), (1, 0)]
HBM = pl.BlockSpec(memory_space=pltpu.HBM)
VMEM = pl.BlockSpec(memory_space=pltpu.VMEM)
PARAMS = pltpu.CompilerParams(vmem_limit_bytes=40 * 1024 * 1024)

LOW_SLOT = N_FR - MARGIN
HIGH_SLOT = N_FR


def dft_tables():
    channel = np.arange(CH).reshape(CH // N_Y, N_Y).T.reshape(-1)
    phase = (channel[:, None] + OFFSET) * np.arange(FRAME)[None, :] % FRAME
    angle = phase * (2.0 * math.pi / FRAME)
    table = np.concatenate([np.cos(angle), -np.sin(angle)], 0) / math.sqrt(FRAME)
    high = table.astype(jnp.bfloat16)
    low = (table - high.astype(np.float64)).astype(jnp.bfloat16)
    return high, low


def dot_t(a, b):
    return lax.dot_general(a, b, (((1,), (1,)), ((), ())), preferred_element_type=jnp.float32)


def lane_ids(rows):
    return lax.broadcasted_iota(jnp.int32, (rows, LANES), 1)


def fetch(pairs, sems):
    copies = [pltpu.make_async_copy(src, dst, sems.at[n]) for n, (src, dst) in enumerate(pairs)]
    for copy in copies:
        copy.start()
    return copies


def run_filter(taps_ref, frame_at, keep, count, block):
    lo = pl.multiple_of(block * LANES, LANES)
    taps = [jnp.broadcast_to(taps_ref[k : k + 1, pl.ds(lo, LANES)], (N_IN, LANES)) for k in range(TAPS)]
    window = []
    for t in range(count + MARGIN):
        window.append(frame_at(t, lo).astype(jnp.float32))
        if t < MARGIN:
            continue
        total = taps[0] * window[0]
        for k in range(1, TAPS):
            total = total + taps[k] * window[k]
        window.pop(0)
        keep(t - MARGIN, total)


def pieces(x):
    high = x.astype(jnp.bfloat16)
    return high, (x - high.astype(jnp.float32)).astype(jnp.bfloat16)


def at(t, lo):
    return pl.ds(pl.multiple_of(t * FRAME + lo, LANES), LANES)


def prefilter_kernel(
    volt_hbm, taps_hbm, high_hbm, low_hbm, fhigh, flow, seam, taps_ref, high_ref, low_ref, frames, filt, sems
):
    core, yhi = lax.axis_index("core"), lax.axis_index("yhi")
    edge = MARGIN * FRAME
    own = N_FR * FRAME
    nothing = jnp.zeros((N_IN, edge), jnp.bfloat16)
    offset = pl.multiple_of((1 - core) * edge, LANES)
    copies = fetch(
        [
            (volt_hbm, frames.at[:, pl.ds(offset, own)]),
            (taps_hbm, taps_ref),
            (high_hbm, high_ref),
            (low_hbm, low_ref),
        ],
        sems,
    )
    tail = pltpu.make_async_copy(volt_hbm.at[:, pl.ds(own - edge, edge)], frames.at[:, pl.ds(own, edge)], sems.at[4])
    second = (core == 1) & (yhi == 0)

    @pl.when(second)
    def _():
        tail.start()

    @pl.when(core == 0)
    def _():
        frames[:, :edge] = nothing

    @pl.when((core == 1) & (yhi == 1))
    def _():
        frames[:, own:] = nothing

    copies[0].wait()
    copies[1].wait()

    @pl.when(second)
    def _():
        tail.wait()

    seam[...] = frames[:, own:]

    @pl.loop(0, FRAME // LANES)
    def _(block):
        def keep(f, x):
            filt[block, f * N_IN : (f + 1) * N_IN, :] = x

        run_filter(taps_ref, lambda t, lo: frames[:, at(t, lo)], keep, N_FR, block)

    for i in range(N_IN):
        for block in range(FRAME // LANES):
            high, low = pieces(filt[block, pl.ds(i, N_FR, stride=N_IN), :])
            fhigh[i * N_FR : (i + 1) * N_FR, block * LANES : (block + 1) * LANES] = high
            flow[i * N_FR : (i + 1) * N_FR, block * LANES : (block + 1) * LANES] = low
    copies[2].wait()
    copies[3].wait()


def channelize_kernel(fhigh, flow, seam, other_ref, taps_ref, high_ref, low_ref, out_ref, filt, ghigh, glow, spread):
    core, yhi = lax.axis_index("core"), lax.axis_index("yhi")
    more = HALF - N_FR
    real_samples = (core == 0) | (yhi == 1)

    def frame_at(t, lo):
        if t < MARGIN:
            return seam[:, at(t, lo)]
        return jnp.where(real_samples, other_ref[:, at(t - MARGIN, lo)].astype(jnp.float32), 0.0)

    @pl.loop(0, FRAME // LANES)
    def _(block):
        def keep(f, x):
            filt[block, f * N_IN : (f + 1) * N_IN, :] = x

        run_filter(taps_ref, frame_at, keep, MARGIN, block)
        filt[block, MARGIN * N_IN :, :] = jnp.zeros(((more - MARGIN) * N_IN, LANES), jnp.float32)

    for i in range(N_IN):
        for block in range(FRAME // LANES):
            high, low = pieces(filt[block, pl.ds(i, more, stride=N_IN), :])
            ghigh[i * more : (i + 1) * more, block * LANES : (block + 1) * LANES] = high
            glow[i * more : (i + 1) * more, block * LANES : (block + 1) * LANES] = low

    lanes = lane_ids(CH)
    slot = lanes % HALF
    drop = (slot < MARGIN) & (core == 0) & (yhi == 1)
    split = (slot >= LOW_SLOT) & (slot < HIGH_SLOT) & (core == 1)

    def rows_of(f, g, i):
        return [f[i * N_FR : (i + 1) * N_FR, :], g[i * more : (i + 1) * more, :]]

    for pair in range(N_IN // 2):
        i = pair * 2
        fh = jnp.concatenate(rows_of(fhigh, ghigh, i) + rows_of(fhigh, ghigh, i + 1), 0)
        fl = jnp.concatenate(rows_of(flow, glow, i) + rows_of(flow, glow, i + 1), 0)
        spec = dot_t(high_ref[...], fh) + (dot_t(high_ref[...], fl) + dot_t(low_ref[...], fh))
        real, imag = spec[:CH], spec[CH:]
        first = jnp.where(lanes < HALF, real, pltpu.roll(imag, HALF, 1))
        second = jnp.where(lanes < HALF, pltpu.roll(real, HALF, 1), imag)
        for sub, value in enumerate((first, second)):
            rest = value - value.astype(jnp.bfloat16).astype(jnp.float32)
            value = jnp.where(split, pltpu.roll(rest, LANES - MARGIN, 1), value)
            value = jnp.where(drop, 0.0, value)
            spread[pl.ds(i + sub, CH, stride=N_IN), :] = value
    result = spread[...].astype(jnp.bfloat16)
    for copy in range(2):
        out_ref[copy * CH * N_IN : (copy + 1) * CH * N_IN, :] = result


def natural(block):
    by_y = block.reshape(N_Y, CH // N_Y, N_IN, LANES)
    return jnp.stack([by_y[y] for y in range(N_Y)], axis=1).reshape(N_INPUTS, LANES)


def lay(in_ref, cols_ref, rows_ref, parts):
    core, yhi = lax.axis_index("core"), lax.axis_index("yhi")
    rows = rows_ref.shape[1]

    @pl.when(jnp.logical_not(parts))
    def _():
        for t in range(2):
            block = natural(in_ref[t * N_INPUTS : (t + 1) * N_INPUTS, :].astype(jnp.float32))
            cols_ref[:, t * LANES : (t + 1) * LANES] = block.astype(jnp.bfloat16)

    @pl.when(parts)
    def _():
        slot = lane_ids(N_INPUTS) % HALF
        edge = (slot >= HIGH_SLOT) & (slot < SLOTS)
        low = (slot >= LOW_SLOT) & (slot < HIGH_SLOT)
        a = in_ref[:N_INPUTS, :].astype(jnp.float32)
        b = in_ref[N_INPUTS:, :].astype(jnp.float32)
        total = (a + pltpu.roll(a, MARGIN, 1)) + (b + pltpu.roll(b, MARGIN, 1))
        one = jnp.where(edge, total, jnp.where(low, 0.0, a))
        two = jnp.where(edge | low, 0.0, b)
        cols_ref[:, :LANES] = natural(one).astype(jnp.bfloat16)
        cols_ref[:, LANES:] = natural(two).astype(jnp.bfloat16)

    own = pl.multiple_of((yhi * 2 + core) * rows, rows)
    lanes = lane_ids(rows)
    for t in range(2):
        x = cols_ref[pl.ds(own, rows), t * LANES : (t + 1) * LANES]
        rows_ref[0, :, t * LANES : (t + 1) * LANES] = x
        turned = pltpu.roll(x.astype(jnp.float32), HALF, 1)
        turned = jnp.where(lanes < HALF, turned, -turned)
        rows_ref[1, :, t * LANES : (t + 1) * LANES] = turned.astype(jnp.bfloat16)


def first_half_kernel(in_ref, part_ref, cols_ref, rows_ref):
    lay(in_ref, cols_ref, rows_ref, lax.axis_index("core") == 1)
    cols = part_ref.shape[3]
    for j in range(part_ref.shape[0]):
        for part in range(2):
            part_ref[j, part] = dot_t(rows_ref[part], cols_ref[j * cols : (j + 1) * cols, :])


def second_half_kernel(scale, in_ref, part_ref, out_hbm, cols_ref, rows_ref, out_ref, sems):
    lay(in_ref, cols_ref, rows_ref, lax.axis_index("core") == 0)
    chunks, _, _, cols = out_ref.shape
    copies = []
    for j in range(chunks):
        cut = slice(j * cols, (j + 1) * cols)
        for part in range(2):
            out_ref[j, part] = (part_ref[j, part] + dot_t(rows_ref[part], cols_ref[cut, :])) * scale
            copy = pltpu.make_async_copy(out_ref.at[j, part], out_hbm.at[part, 0, :, cut], sems.at[j, part])
            copy.start()
            copies.append(copy)
    for copy in copies:
        copy.wait()


def far_memory(x):
    return pltpu.with_memory_space_constraint(x, pltpu.HBM)


def per_device(voltages, fir_taps):
    other = lax.ppermute(voltages, "core", SWAP)
    high, low = (jnp.asarray(table) for table in dft_tables())
    seam_shape = (N_IN, MARGIN * FRAME)
    fhigh, flow, seam, taps, high, low = pl.pallas_call(
        prefilter_kernel,
        out_shape=[
            jax.ShapeDtypeStruct((N_IN * N_FR, FRAME), jnp.bfloat16),
            jax.ShapeDtypeStruct((N_IN * N_FR, FRAME), jnp.bfloat16),
            jax.ShapeDtypeStruct(seam_shape, jnp.bfloat16),
            jax.ShapeDtypeStruct(fir_taps.shape, jnp.float32),
            jax.ShapeDtypeStruct(high.shape, jnp.bfloat16),
            jax.ShapeDtypeStruct(low.shape, jnp.bfloat16),
        ],
        in_specs=[HBM] * 4,
        out_specs=[VMEM] * 6,
        scratch_shapes=[
            pltpu.VMEM((N_IN, SLOTS * FRAME), jnp.bfloat16),
            pltpu.VMEM((FRAME // LANES, N_FR * N_IN, LANES), jnp.float32),
            pltpu.SemaphoreType.DMA((5,)),
        ],
        compiler_params=PARAMS,
        cost_estimate=pl.CostEstimate(flops=10**8, bytes_accessed=4 * 10**6, transcendentals=0),
        name="prefilter",
    )(*(far_memory(x) for x in (voltages, fir_taps, high, low)))
    more = HALF - N_FR
    spectra = pl.pallas_call(
        channelize_kernel,
        out_shape=jax.ShapeDtypeStruct((2 * CH * N_IN, LANES), jnp.bfloat16),
        in_specs=[VMEM] * 7,
        out_specs=VMEM,
        scratch_shapes=[
            pltpu.VMEM((FRAME // LANES, more * N_IN, LANES), jnp.float32),
            pltpu.VMEM((more * N_IN, FRAME), jnp.bfloat16),
            pltpu.VMEM((more * N_IN, FRAME), jnp.bfloat16),
            pltpu.VMEM((CH * N_IN, LANES), jnp.float32),
        ],
        compiler_params=PARAMS,
        name="channelize",
    )(fhigh, flow, seam, other, taps, high, low)
    turned = lax.all_to_all(
        spectra.reshape(2 * CH, N_IN, LANES), ("yhi", "ylo", "z", "x"), 0, 0, tiled=True
    )
    own = turned.reshape(2 * N_INPUTS, LANES)
    other_core = lax.ppermute(own, "core", SWAP)
    rows = N_INPUTS // N_TB
    cols = 256
    chunks = N_INPUTS // cols
    operands = [
        pltpu.VMEM((N_INPUTS, 2 * LANES), jnp.bfloat16),
        pltpu.VMEM((2, rows, 2 * LANES), jnp.bfloat16),
    ]
    half = pl.pallas_call(
        first_half_kernel,
        out_shape=jax.ShapeDtypeStruct((chunks, 2, rows, cols), jnp.float32),
        in_specs=[VMEM],
        out_specs=VMEM,
        scratch_shapes=operands,
        compiler_params=PARAMS,
        cost_estimate=pl.CostEstimate(flops=3 * 10**8, bytes_accessed=3 * 10**6, transcendentals=0),
        name="first_half",
    )(own)
    scale = np.float32(1.0 / (N_FR * N_TB))
    return pl.pallas_call(
        lambda *refs: second_half_kernel(scale, *refs),
        out_shape=jax.ShapeDtypeStruct((2, 1, rows, N_INPUTS), jnp.float32),
        in_specs=[VMEM, VMEM],
        out_specs=HBM,
        scratch_shapes=operands
        + [
            pltpu.VMEM((chunks, 2, rows, cols), jnp.float32),
            pltpu.SemaphoreType.DMA((chunks, 2)),
        ],
        compiler_params=PARAMS,
        name="second_half",
    )(other_core, half)


def solution(mesh):
    fine = Mesh(mesh.devices.reshape(8, 4, 4, 2, 2), ("z", "x", "ylo", "yhi", "core"))
    in_specs = (P(("z", "x", "ylo"), ("yhi", "core")), P())
    out_specs = P(None, ("z", "x", "ylo"), ("yhi", "core"), None)
    return jax.shard_map(
        per_device, mesh=fine, in_specs=in_specs, out_specs=out_specs, check_vma=False
    )
```

```python
import math

import jax
import jax.numpy as jnp
import numpy as np
from jax import lax
from jax.experimental import pallas as pl
from jax.experimental.pallas import tpu as pltpu
from jax.sharding import Mesh
from jax.sharding import PartitionSpec as P

CH = 128
OFFSET = 64
FRAME = 512
TAPS = 12
MARGIN = TAPS - 1
N_IN = 8
N_FR = 48
N_TB = 4
SIZES = (8, 4, 4, 2, 2)
AXES = ("z", "x", "ylo", "yhi", "core")
SLOTS = N_FR + MARGIN
HALF = 64
LANES = 128
N_INPUTS = 1024
SWAP = [(0, 1), (1, 0)]
HBM = pl.BlockSpec(memory_space=pltpu.HBM)
VMEM = pl.BlockSpec(memory_space=pltpu.VMEM)
PARAMS = pltpu.CompilerParams(vmem_limit_bytes=40 * 1024 * 1024)

LOW_SLOT = N_FR - MARGIN
HIGH_SLOT = N_FR
SEED = 1


def listing():
    y, z, x = np.meshgrid(np.arange(8), np.arange(8), np.arange(4), indexing="ij")
    owners = np.stack([y // 4, (z * 4 + x) * 4 + y % 4], -1).reshape(-1, 2)
    return owners[np.random.RandomState(SEED).permutation(2 * CH)]


OWNERS = listing()
PLACE = np.zeros((2, CH), np.int64)
PLACE[OWNERS[:, 0], OWNERS[:, 1]] = np.arange(2 * CH)


def groups():
    yhi, station = OWNERS[:, 0], OWNERS[:, 1]
    return [[int(p) for p in (station * 2 + yhi) * 2 + core] for core in range(2)]


def dft_tables():
    phase = (np.arange(CH)[:, None] + OFFSET) * np.arange(FRAME)[None, :] % FRAME
    angle = phase * (2.0 * math.pi / FRAME)
    table = np.concatenate([np.cos(angle), -np.sin(angle)], 0) / math.sqrt(FRAME)
    high = table.astype(jnp.bfloat16)
    low = (table - high.astype(np.float64)).astype(jnp.bfloat16)
    return high, low


def dot_t(a, b):
    return lax.dot_general(a, b, (((1,), (1,)), ((), ())), preferred_element_type=jnp.float32)


def lane_ids(rows):
    return lax.broadcasted_iota(jnp.int32, (rows, LANES), 1)


def fetch(pairs, sems):
    copies = [pltpu.make_async_copy(src, dst, sems.at[n]) for n, (src, dst) in enumerate(pairs)]
    for copy in copies:
        copy.start()
    return copies


def run_filter(taps_ref, frame_at, keep, count, block):
    lo = pl.multiple_of(block * LANES, LANES)
    taps = [jnp.broadcast_to(taps_ref[k : k + 1, pl.ds(lo, LANES)], (N_IN, LANES)) for k in range(TAPS)]
    window = []
    for t in range(count + MARGIN):
        window.append(frame_at(t, lo).astype(jnp.float32))
        if t < MARGIN:
            continue
        total = taps[0] * window[0]
        for k in range(1, TAPS):
            total = total + taps[k] * window[k]
        window.pop(0)
        keep(t - MARGIN, total)


def pieces(x):
    high = x.astype(jnp.bfloat16)
    return high, (x - high.astype(jnp.float32)).astype(jnp.bfloat16)


def at(t, lo):
    return pl.ds(pl.multiple_of(t * FRAME + lo, LANES), LANES)


def prefilter_kernel(
    volt_hbm, taps_hbm, high_hbm, low_hbm, fhigh, flow, seam, taps_ref, high_ref, low_ref, frames, filt, sems
):
    core, yhi = lax.axis_index("core"), lax.axis_index("yhi")
    edge = MARGIN * FRAME
    own = N_FR * FRAME
    nothing = jnp.zeros((N_IN, edge), jnp.bfloat16)
    offset = pl.multiple_of((1 - core) * edge, LANES)
    copies = fetch(
        [
            (volt_hbm, frames.at[:, pl.ds(offset, own)]),
            (taps_hbm, taps_ref),
            (high_hbm, high_ref),
            (low_hbm, low_ref),
        ],
        sems,
    )
    tail = pltpu.make_async_copy(volt_hbm.at[:, pl.ds(own - edge, edge)], frames.at[:, pl.ds(own, edge)], sems.at[4])
    second = (core == 1) & (yhi == 0)

    @pl.when(second)
    def _():
        tail.start()

    @pl.when(core == 0)
    def _():
        frames[:, :edge] = nothing

    @pl.when((core == 1) & (yhi == 1))
    def _():
        frames[:, own:] = nothing

    copies[0].wait()
    copies[1].wait()

    @pl.when(second)
    def _():
        tail.wait()

    seam[...] = frames[:, own:]

    @pl.loop(0, FRAME // LANES)
    def _(block):
        def keep(f, x):
            filt[block, f * N_IN : (f + 1) * N_IN, :] = x

        run_filter(taps_ref, lambda t, lo: frames[:, at(t, lo)], keep, N_FR, block)

    for i in range(N_IN):
        for block in range(FRAME // LANES):
            high, low = pieces(filt[block, pl.ds(i, N_FR, stride=N_IN), :])
            fhigh[i * N_FR : (i + 1) * N_FR, block * LANES : (block + 1) * LANES] = high
            flow[i * N_FR : (i + 1) * N_FR, block * LANES : (block + 1) * LANES] = low
    copies[2].wait()
    copies[3].wait()


def channelize_kernel(fhigh, flow, seam, other_ref, taps_ref, high_ref, low_ref, out_ref, filt, ghigh, glow, spread):
    core, yhi = lax.axis_index("core"), lax.axis_index("yhi")
    more = HALF - N_FR
    real_samples = (core == 0) | (yhi == 1)

    def frame_at(t, lo):
        if t < MARGIN:
            return seam[:, at(t, lo)]
        return jnp.where(real_samples, other_ref[:, at(t - MARGIN, lo)].astype(jnp.float32), 0.0)

    @pl.loop(0, FRAME // LANES)
    def _(block):
        def keep(f, x):
            filt[block, f * N_IN : (f + 1) * N_IN, :] = x

        run_filter(taps_ref, frame_at, keep, MARGIN, block)
        filt[block, MARGIN * N_IN :, :] = jnp.zeros(((more - MARGIN) * N_IN, LANES), jnp.float32)

    for i in range(N_IN):
        for block in range(FRAME // LANES):
            high, low = pieces(filt[block, pl.ds(i, more, stride=N_IN), :])
            ghigh[i * more : (i + 1) * more, block * LANES : (block + 1) * LANES] = high
            glow[i * more : (i + 1) * more, block * LANES : (block + 1) * LANES] = low

    lanes = lane_ids(CH)
    slot = lanes % HALF
    drop = (slot < MARGIN) & (core == 0) & (yhi == 1)
    split = (slot >= LOW_SLOT) & (slot < HIGH_SLOT) & (core == 1)

    def rows_of(f, g, i):
        return [f[i * N_FR : (i + 1) * N_FR, :], g[i * more : (i + 1) * more, :]]

    for pair in range(N_IN // 2):
        i = pair * 2
        fh = jnp.concatenate(rows_of(fhigh, ghigh, i) + rows_of(fhigh, ghigh, i + 1), 0)
        fl = jnp.concatenate(rows_of(flow, glow, i) + rows_of(flow, glow, i + 1), 0)
        spec = dot_t(high_ref[...], fh) + (dot_t(high_ref[...], fl) + dot_t(low_ref[...], fh))
        real, imag = spec[:CH], spec[CH:]
        first = jnp.where(lanes < HALF, real, pltpu.roll(imag, HALF, 1))
        second = jnp.where(lanes < HALF, pltpu.roll(real, HALF, 1), imag)
        for sub, value in enumerate((first, second)):
            rest = value - value.astype(jnp.bfloat16).astype(jnp.float32)
            value = jnp.where(split, pltpu.roll(rest, LANES - MARGIN, 1), value)
            value = jnp.where(drop, 0.0, value)
            spread[pl.ds(i + sub, CH, stride=N_IN), :] = value
    for pair in range(CH):
        two = [spread[int(c) * N_IN : (int(c) + 1) * N_IN, :] for c in OWNERS[2 * pair : 2 * pair + 2, 1]]
        out_ref[pair * 2 * N_IN : (pair + 1) * 2 * N_IN, :] = jnp.concatenate(two, 0).astype(jnp.bfloat16)


def two_tiles(in_ref, yhi, pair):
    tiles = []
    for place in PLACE[yhi, 2 * pair : 2 * pair + 2]:
        both = in_ref[int(place) // 2 * 2 * N_IN : (int(place) // 2 + 1) * 2 * N_IN, :].astype(jnp.float32)
        tiles.append(both[int(place) % 2 * N_IN : (int(place) % 2 + 1) * N_IN])
    return jnp.concatenate(tiles, 0)


def lay(in_ref, cols_ref, rows_ref, parts):
    core, yhi = lax.axis_index("core"), lax.axis_index("yhi")
    rows = rows_ref.shape[1]
    step = 2 * N_IN

    @pl.when(jnp.logical_not(parts))
    def _():
        for pair in range(CH // 2):
            for t in range(2):
                value = two_tiles(in_ref, t, pair).astype(jnp.bfloat16)
                cols_ref[pair * step : (pair + 1) * step, t * LANES : (t + 1) * LANES] = value

    @pl.when(parts)
    def _():
        slot = lane_ids(step) % HALF
        edge = (slot >= HIGH_SLOT) & (slot < SLOTS)
        low = (slot >= LOW_SLOT) & (slot < HIGH_SLOT)
        for pair in range(CH // 2):
            a, b = two_tiles(in_ref, 0, pair), two_tiles(in_ref, 1, pair)
            total = (a + pltpu.roll(a, MARGIN, 1)) + (b + pltpu.roll(b, MARGIN, 1))
            one = jnp.where(edge, total, jnp.where(low, 0.0, a))
            two = jnp.where(edge | low, 0.0, b)
            cut = slice(pair * step, (pair + 1) * step)
            cols_ref[cut, :LANES] = one.astype(jnp.bfloat16)
            cols_ref[cut, LANES:] = two.astype(jnp.bfloat16)

    own = pl.multiple_of((yhi * 2 + core) * rows, rows)
    lanes = lane_ids(rows)
    for t in range(2):
        x = cols_ref[pl.ds(own, rows), t * LANES : (t + 1) * LANES]
        rows_ref[0, :, t * LANES : (t + 1) * LANES] = x
        turned = pltpu.roll(x.astype(jnp.float32), HALF, 1)
        turned = jnp.where(lanes < HALF, turned, -turned)
        rows_ref[1, :, t * LANES : (t + 1) * LANES] = turned.astype(jnp.bfloat16)


def first_half_kernel(in_ref, part_ref, cols_ref, rows_ref):
    lay(in_ref, cols_ref, rows_ref, lax.axis_index("core") == 1)
    cols = part_ref.shape[3]
    for j in range(part_ref.shape[0]):
        for part in range(2):
            part_ref[j, part] = dot_t(rows_ref[part], cols_ref[j * cols : (j + 1) * cols, :])


def second_half_kernel(scale, in_ref, part_ref, out_hbm, cols_ref, rows_ref, out_ref, sems):
    lay(in_ref, cols_ref, rows_ref, lax.axis_index("core") == 0)
    chunks, _, _, cols = out_ref.shape
    copies = []
    for j in range(chunks):
        cut = slice(j * cols, (j + 1) * cols)
        for part in range(2):
            out_ref[j, part] = (part_ref[j, part] + dot_t(rows_ref[part], cols_ref[cut, :])) * scale
            copy = pltpu.make_async_copy(out_ref.at[j, part], out_hbm.at[part, 0, :, cut], sems.at[j, part])
            copy.start()
            copies.append(copy)
    for copy in copies:
        copy.wait()


def far_memory(x):
    return pltpu.with_memory_space_constraint(x, pltpu.HBM)


def per_device(voltages, fir_taps):
    other = lax.ppermute(voltages, "core", SWAP)
    high, low = (jnp.asarray(table) for table in dft_tables())
    seam_shape = (N_IN, MARGIN * FRAME)
    fhigh, flow, seam, taps, high, low = pl.pallas_call(
        prefilter_kernel,
        out_shape=[
            jax.ShapeDtypeStruct((N_IN * N_FR, FRAME), jnp.bfloat16),
            jax.ShapeDtypeStruct((N_IN * N_FR, FRAME), jnp.bfloat16),
            jax.ShapeDtypeStruct(seam_shape, jnp.bfloat16),
            jax.ShapeDtypeStruct(fir_taps.shape, jnp.float32),
            jax.ShapeDtypeStruct(high.shape, jnp.bfloat16),
            jax.ShapeDtypeStruct(low.shape, jnp.bfloat16),
        ],
        in_specs=[HBM] * 4,
        out_specs=[VMEM] * 6,
        scratch_shapes=[
            pltpu.VMEM((N_IN, SLOTS * FRAME), jnp.bfloat16),
            pltpu.VMEM((FRAME // LANES, N_FR * N_IN, LANES), jnp.float32),
            pltpu.SemaphoreType.DMA((5,)),
        ],
        compiler_params=PARAMS,
        cost_estimate=pl.CostEstimate(flops=10**8, bytes_accessed=4 * 10**6, transcendentals=0),
        name="prefilter",
    )(*(far_memory(x) for x in (voltages, fir_taps, high, low)))
    more = HALF - N_FR
    spectra = pl.pallas_call(
        channelize_kernel,
        out_shape=jax.ShapeDtypeStruct((2 * CH * N_IN, LANES), jnp.bfloat16),
        in_specs=[VMEM] * 7,
        out_specs=VMEM,
        scratch_shapes=[
            pltpu.VMEM((FRAME // LANES, more * N_IN, LANES), jnp.float32),
            pltpu.VMEM((more * N_IN, FRAME), jnp.bfloat16),
            pltpu.VMEM((more * N_IN, FRAME), jnp.bfloat16),
            pltpu.VMEM((CH * N_IN, LANES), jnp.float32),
        ],
        compiler_params=PARAMS,
        name="channelize",
    )(fhigh, flow, seam, other, taps, high, low)
    turned = lax.all_to_all(
        spectra.reshape(2 * CH, N_IN, LANES), AXES, 0, 0, axis_index_groups=groups(), tiled=True
    )
    own = turned.reshape(2 * N_INPUTS, LANES)
    other_core = lax.ppermute(own, "core", SWAP)
    rows = N_INPUTS // N_TB
    cols = 256
    chunks = N_INPUTS // cols
    operands = [
        pltpu.VMEM((N_INPUTS, 2 * LANES), jnp.bfloat16),
        pltpu.VMEM((2, rows, 2 * LANES), jnp.bfloat16),
    ]
    half = pl.pallas_call(
        first_half_kernel,
        out_shape=jax.ShapeDtypeStruct((chunks, 2, rows, cols), jnp.float32),
        in_specs=[VMEM],
        out_specs=VMEM,
        scratch_shapes=operands,
        compiler_params=PARAMS,
        cost_estimate=pl.CostEstimate(flops=3 * 10**8, bytes_accessed=3 * 10**6, transcendentals=0),
        name="first_half",
    )(own)
    scale = np.float32(1.0 / (N_FR * N_TB))
    return pl.pallas_call(
        lambda *refs: second_half_kernel(scale, *refs),
        out_shape=jax.ShapeDtypeStruct((2, 1, rows, N_INPUTS), jnp.float32),
        in_specs=[VMEM, VMEM],
        out_specs=HBM,
        scratch_shapes=operands
        + [
            pltpu.VMEM((chunks, 2, rows, cols), jnp.float32),
            pltpu.SemaphoreType.DMA((chunks, 2)),
        ],
        compiler_params=PARAMS,
        name="second_half",
    )(other_core, half)


def solution(mesh):
    fine = Mesh(mesh.devices.reshape(SIZES), AXES)
    in_specs = (P(("z", "x", "ylo"), ("yhi", "core")), P())
    out_specs = P(None, ("z", "x", "ylo"), ("yhi", "core"), None)
    return jax.shard_map(
        per_device, mesh=fine, in_specs=in_specs, out_specs=out_specs, check_vma=False
    )
```

```python
import math

import jax
import jax.numpy as jnp
import numpy as np
from jax import lax
from jax.experimental import pallas as pl
from jax.experimental.pallas import tpu as pltpu
from jax.sharding import Mesh
from jax.sharding import PartitionSpec as P

CH = 128
OFFSET = 64
FRAME = 512
TAPS = 12
MARGIN = TAPS - 1
N_IN = 8
N_FR = 48
N_TB = 4
SIZES = (8, 4, 4, 2, 2)
AXES = ("z", "x", "ylo", "yhi", "core")
SLOTS = N_FR + MARGIN
HALF = 64
LANES = 128
N_INPUTS = 1024
SWAP = [(0, 1), (1, 0)]
HBM = pl.BlockSpec(memory_space=pltpu.HBM)
VMEM = pl.BlockSpec(memory_space=pltpu.VMEM)
PARAMS = pltpu.CompilerParams(vmem_limit_bytes=40 * 1024 * 1024)

LOW_SLOT = N_FR - MARGIN
HIGH_SLOT = N_FR
SEED = 8


def listing():
    y, z, x = np.meshgrid(np.arange(8), np.arange(8), np.arange(4), indexing="ij")
    owners = np.stack([y // 4, (z * 4 + x) * 4 + y % 4], -1).reshape(-1, 2)
    return owners[np.random.RandomState(SEED).permutation(2 * CH)]


OWNERS = listing()
PLACE = np.zeros((2, CH), np.int64)
PLACE[OWNERS[:, 0], OWNERS[:, 1]] = np.arange(2 * CH)


def groups():
    yhi, station = OWNERS[:, 0], OWNERS[:, 1]
    return [[int(p) for p in (station * 2 + yhi) * 2 + core] for core in range(2)]


def dft_tables():
    phase = (np.arange(CH)[:, None] + OFFSET) * np.arange(FRAME)[None, :] % FRAME
    angle = phase * (2.0 * math.pi / FRAME)
    table = np.concatenate([np.cos(angle), -np.sin(angle)], 0) / math.sqrt(FRAME)
    high = table.astype(jnp.bfloat16)
    low = (table - high.astype(np.float64)).astype(jnp.bfloat16)
    return high, low


def dot_t(a, b):
    return lax.dot_general(a, b, (((1,), (1,)), ((), ())), preferred_element_type=jnp.float32)


def lane_ids(rows):
    return lax.broadcasted_iota(jnp.int32, (rows, LANES), 1)


def fetch(pairs, sems):
    copies = [pltpu.make_async_copy(src, dst, sems.at[n]) for n, (src, dst) in enumerate(pairs)]
    for copy in copies:
        copy.start()
    return copies


def run_filter(taps_ref, frame_at, keep, count, block):
    lo = block * LANES if isinstance(block, int) else pl.multiple_of(block * LANES, LANES)
    taps = [jnp.broadcast_to(taps_ref[k : k + 1, pl.ds(lo, LANES)], (N_IN, LANES)) for k in range(TAPS)]
    window = []
    for t in range(count + MARGIN):
        window.append(frame_at(t, lo).astype(jnp.float32))
        if t < MARGIN:
            continue
        total = taps[0] * window[0]
        for k in range(1, TAPS):
            total = total + taps[k] * window[k]
        window.pop(0)
        keep(t - MARGIN, total)


def pieces(x):
    high = x.astype(jnp.bfloat16)
    return high, (x - high.astype(jnp.float32)).astype(jnp.bfloat16)


def at(t, lo):
    if isinstance(lo, int):
        return slice(t * FRAME + lo, t * FRAME + lo + LANES)
    return pl.ds(pl.multiple_of(t * FRAME + lo, LANES), LANES)


def prefilter_kernel(
    volt_hbm, taps_hbm, high_hbm, low_hbm, fhigh, flow, seam, taps_ref, high_ref, low_ref, frames, filt, sems
):
    core, yhi = lax.axis_index("core"), lax.axis_index("yhi")
    edge = MARGIN * FRAME
    own = N_FR * FRAME
    nothing = jnp.zeros((N_IN, edge), jnp.bfloat16)
    offset = pl.multiple_of((1 - core) * edge, LANES)
    copies = fetch(
        [
            (volt_hbm, frames.at[:, pl.ds(offset, own)]),
            (taps_hbm, taps_ref),
            (high_hbm, high_ref),
            (low_hbm, low_ref),
        ],
        sems,
    )
    tail = pltpu.make_async_copy(volt_hbm.at[:, pl.ds(own - edge, edge)], frames.at[:, pl.ds(own, edge)], sems.at[4])
    second = (core == 1) & (yhi == 0)

    @pl.when(second)
    def _():
        tail.start()

    @pl.when(core == 0)
    def _():
        frames[:, :edge] = nothing

    @pl.when((core == 1) & (yhi == 1))
    def _():
        frames[:, own:] = nothing

    copies[0].wait()
    copies[1].wait()

    @pl.when(second)
    def _():
        tail.wait()

    seam[...] = frames[:, own:]

    for block in range(FRAME // LANES):
        def keep(f, x, block=block):
            filt[block, f * N_IN : (f + 1) * N_IN, :] = x

        run_filter(taps_ref, lambda t, lo: frames[:, at(t, lo)], keep, N_FR, block)

    for i in range(N_IN):
        for block in range(FRAME // LANES):
            high, low = pieces(filt[block, pl.ds(i, N_FR, stride=N_IN), :])
            fhigh[i * N_FR : (i + 1) * N_FR, block * LANES : (block + 1) * LANES] = high
            flow[i * N_FR : (i + 1) * N_FR, block * LANES : (block + 1) * LANES] = low
    copies[2].wait()
    copies[3].wait()


def channelize_kernel(fhigh, flow, seam, other_ref, taps_ref, high_ref, low_ref, out_ref, filt, ghigh, glow, spread):
    core, yhi = lax.axis_index("core"), lax.axis_index("yhi")
    more = HALF - N_FR
    real_samples = (core == 0) | (yhi == 1)

    def frame_at(t, lo):
        if t < MARGIN:
            return seam[:, at(t, lo)]
        return jnp.where(real_samples, other_ref[:, at(t - MARGIN, lo)].astype(jnp.float32), 0.0)

    for block in range(FRAME // LANES):
        def keep(f, x, block=block):
            filt[block, f * N_IN : (f + 1) * N_IN, :] = x

        run_filter(taps_ref, frame_at, keep, MARGIN, block)
        filt[block, MARGIN * N_IN :, :] = jnp.zeros(((more - MARGIN) * N_IN, LANES), jnp.float32)

    for i in range(N_IN):
        for block in range(FRAME // LANES):
            high, low = pieces(filt[block, pl.ds(i, more, stride=N_IN), :])
            ghigh[i * more : (i + 1) * more, block * LANES : (block + 1) * LANES] = high
            glow[i * more : (i + 1) * more, block * LANES : (block + 1) * LANES] = low

    lanes = lane_ids(CH)
    slot = lanes % HALF
    drop = (slot < MARGIN) & (core == 0) & (yhi == 1)
    split = (slot >= LOW_SLOT) & (slot < HIGH_SLOT) & (core == 1)

    def rows_of(f, g, i):
        return [f[i * N_FR : (i + 1) * N_FR, :], g[i * more : (i + 1) * more, :]]

    for pair in range(N_IN // 2):
        i = pair * 2
        fh = jnp.concatenate(rows_of(fhigh, ghigh, i) + rows_of(fhigh, ghigh, i + 1), 0)
        fl = jnp.concatenate(rows_of(flow, glow, i) + rows_of(flow, glow, i + 1), 0)
        spec = dot_t(high_ref[...], fh) + (dot_t(high_ref[...], fl) + dot_t(low_ref[...], fh))
        real, imag = spec[:CH], spec[CH:]
        first = jnp.where(lanes < HALF, real, pltpu.roll(imag, HALF, 1))
        second = jnp.where(lanes < HALF, pltpu.roll(real, HALF, 1), imag)
        for sub, value in enumerate((first, second)):
            rest = value - value.astype(jnp.bfloat16).astype(jnp.float32)
            value = jnp.where(split, pltpu.roll(rest, LANES - MARGIN, 1), value)
            value = jnp.where(drop, 0.0, value)
            spread[pl.ds(i + sub, CH, stride=N_IN), :] = value
    for pair in range(CH):
        two = [spread[int(c) * N_IN : (int(c) + 1) * N_IN, :] for c in OWNERS[2 * pair : 2 * pair + 2, 1]]
        out_ref[pair * 2 * N_IN : (pair + 1) * 2 * N_IN, :] = jnp.concatenate(two, 0).astype(jnp.bfloat16)


def two_tiles(in_ref, yhi, pair):
    tiles = []
    for place in PLACE[yhi, 2 * pair : 2 * pair + 2]:
        both = in_ref[int(place) // 2 * 2 * N_IN : (int(place) // 2 + 1) * 2 * N_IN, :].astype(jnp.float32)
        tiles.append(both[int(place) % 2 * N_IN : (int(place) % 2 + 1) * N_IN])
    return jnp.concatenate(tiles, 0)


def lay(in_ref, cols_ref, rows_ref, parts):
    core, yhi = lax.axis_index("core"), lax.axis_index("yhi")
    rows = rows_ref.shape[1]
    step = 2 * N_IN

    @pl.when(jnp.logical_not(parts))
    def _():
        for pair in range(CH // 2):
            for t in range(2):
                value = two_tiles(in_ref, t, pair).astype(jnp.bfloat16)
                cols_ref[pair * step : (pair + 1) * step, t * LANES : (t + 1) * LANES] = value

    @pl.when(parts)
    def _():
        slot = lane_ids(step) % HALF
        edge = (slot >= HIGH_SLOT) & (slot < SLOTS)
        low = (slot >= LOW_SLOT) & (slot < HIGH_SLOT)
        for pair in range(CH // 2):
            a, b = two_tiles(in_ref, 0, pair), two_tiles(in_ref, 1, pair)
            total = (a + pltpu.roll(a, MARGIN, 1)) + (b + pltpu.roll(b, MARGIN, 1))
            one = jnp.where(edge, total, jnp.where(low, 0.0, a))
            two = jnp.where(edge | low, 0.0, b)
            cut = slice(pair * step, (pair + 1) * step)
            cols_ref[cut, :LANES] = one.astype(jnp.bfloat16)
            cols_ref[cut, LANES:] = two.astype(jnp.bfloat16)

    own = pl.multiple_of((yhi * 2 + core) * rows, rows)
    lanes = lane_ids(rows)
    for t in range(2):
        x = cols_ref[pl.ds(own, rows), t * LANES : (t + 1) * LANES]
        rows_ref[0, :, t * LANES : (t + 1) * LANES] = x
        turned = pltpu.roll(x.astype(jnp.float32), HALF, 1)
        turned = jnp.where(lanes < HALF, turned, -turned)
        rows_ref[1, :, t * LANES : (t + 1) * LANES] = turned.astype(jnp.bfloat16)


def first_half_kernel(in_ref, part_ref, cols_ref, rows_ref):
    lay(in_ref, cols_ref, rows_ref, lax.axis_index("core") == 1)
    cols = part_ref.shape[3]
    for j in range(part_ref.shape[0]):
        for part in range(2):
            part_ref[j, part] = dot_t(rows_ref[part], cols_ref[j * cols : (j + 1) * cols, :])


def second_half_kernel(scale, in_ref, part_ref, out_hbm, cols_ref, rows_ref, out_ref, sems):
    lay(in_ref, cols_ref, rows_ref, lax.axis_index("core") == 0)
    chunks, _, _, cols = out_ref.shape
    copies = []
    for j in range(chunks):
        cut = slice(j * cols, (j + 1) * cols)
        for part in range(2):
            out_ref[j, part] = (part_ref[j, part] + dot_t(rows_ref[part], cols_ref[cut, :])) * scale
            copy = pltpu.make_async_copy(out_ref.at[j, part], out_hbm.at[part, 0, :, cut], sems.at[j, part])
            copy.start()
            copies.append(copy)
    for copy in copies:
        copy.wait()


def far_memory(x):
    return pltpu.with_memory_space_constraint(x, pltpu.HBM)


def per_device(voltages, fir_taps):
    other = lax.ppermute(voltages, "core", SWAP)
    high, low = (jnp.asarray(table) for table in dft_tables())
    seam_shape = (N_IN, MARGIN * FRAME)
    fhigh, flow, seam, taps, high, low = pl.pallas_call(
        prefilter_kernel,
        out_shape=[
            jax.ShapeDtypeStruct((N_IN * N_FR, FRAME), jnp.bfloat16),
            jax.ShapeDtypeStruct((N_IN * N_FR, FRAME), jnp.bfloat16),
            jax.ShapeDtypeStruct(seam_shape, jnp.bfloat16),
            jax.ShapeDtypeStruct(fir_taps.shape, jnp.float32),
            jax.ShapeDtypeStruct(high.shape, jnp.bfloat16),
            jax.ShapeDtypeStruct(low.shape, jnp.bfloat16),
        ],
        in_specs=[HBM] * 4,
        out_specs=[VMEM] * 6,
        scratch_shapes=[
            pltpu.VMEM((N_IN, SLOTS * FRAME), jnp.bfloat16),
            pltpu.VMEM((FRAME // LANES, N_FR * N_IN, LANES), jnp.float32),
            pltpu.SemaphoreType.DMA((5,)),
        ],
        compiler_params=PARAMS,
        cost_estimate=pl.CostEstimate(flops=10**8, bytes_accessed=4 * 10**6, transcendentals=0),
        name="prefilter",
    )(*(far_memory(x) for x in (voltages, fir_taps, high, low)))
    more = HALF - N_FR
    spectra = pl.pallas_call(
        channelize_kernel,
        out_shape=jax.ShapeDtypeStruct((2 * CH * N_IN, LANES), jnp.bfloat16),
        in_specs=[VMEM] * 7,
        out_specs=VMEM,
        scratch_shapes=[
            pltpu.VMEM((FRAME // LANES, more * N_IN, LANES), jnp.float32),
            pltpu.VMEM((more * N_IN, FRAME), jnp.bfloat16),
            pltpu.VMEM((more * N_IN, FRAME), jnp.bfloat16),
            pltpu.VMEM((CH * N_IN, LANES), jnp.float32),
        ],
        compiler_params=PARAMS,
        name="channelize",
    )(fhigh, flow, seam, other, taps, high, low)
    turned = lax.all_to_all(
        spectra.reshape(2 * CH, N_IN, LANES), AXES, 0, 0, axis_index_groups=groups(), tiled=True
    )
    own = turned.reshape(2 * N_INPUTS, LANES)
    other_core = lax.ppermute(own, "core", SWAP)
    rows = N_INPUTS // N_TB
    cols = 256
    chunks = N_INPUTS // cols
    operands = [
        pltpu.VMEM((N_INPUTS, 2 * LANES), jnp.bfloat16),
        pltpu.VMEM((2, rows, 2 * LANES), jnp.bfloat16),
    ]
    half = pl.pallas_call(
        first_half_kernel,
        out_shape=jax.ShapeDtypeStruct((chunks, 2, rows, cols), jnp.float32),
        in_specs=[VMEM],
        out_specs=VMEM,
        scratch_shapes=operands,
        compiler_params=PARAMS,
        cost_estimate=pl.CostEstimate(flops=3 * 10**8, bytes_accessed=3 * 10**6, transcendentals=0),
        name="first_half",
    )(own)
    scale = np.float32(1.0 / (N_FR * N_TB))
    return pl.pallas_call(
        lambda *refs: second_half_kernel(scale, *refs),
        out_shape=jax.ShapeDtypeStruct((2, 1, rows, N_INPUTS), jnp.float32),
        in_specs=[VMEM, VMEM],
        out_specs=HBM,
        scratch_shapes=operands
        + [
            pltpu.VMEM((chunks, 2, rows, cols), jnp.float32),
            pltpu.SemaphoreType.DMA((chunks, 2)),
        ],
        compiler_params=PARAMS,
        name="second_half",
    )(other_core, half)


def solution(mesh):
    fine = Mesh(mesh.devices.reshape(SIZES), AXES)
    in_specs = (P(("z", "x", "ylo"), ("yhi", "core")), P())
    out_specs = P(None, ("z", "x", "ylo"), ("yhi", "core"), None)
    return jax.shard_map(
        per_device, mesh=fine, in_specs=in_specs, out_specs=out_specs, check_vma=False
    )
```

```python
import math

import jax
import jax.numpy as jnp
import numpy as np
from jax import lax
from jax.experimental import pallas as pl
from jax.experimental.pallas import tpu as pltpu
from jax.sharding import Mesh
from jax.sharding import PartitionSpec as P

CH = 128
OFFSET = 64
FRAME = 512
TAPS = 12
MARGIN = TAPS - 1
N_IN = 8
N_FR = 48
N_TB = 4
SIZES = (8, 4, 4, 2, 2)
AXES = ("z", "x", "ylo", "yhi", "core")
SLOTS = N_FR + MARGIN
HALF = 64
LANES = 128
N_INPUTS = 1024
SWAP = [(0, 1), (1, 0)]
HBM = pl.BlockSpec(memory_space=pltpu.HBM)
VMEM = pl.BlockSpec(memory_space=pltpu.VMEM)
PARAMS = pltpu.CompilerParams(vmem_limit_bytes=40 * 1024 * 1024)

LOW_SLOT = N_FR - MARGIN
HIGH_SLOT = N_FR
SEED = 8


def listing():
    y, z, x = np.meshgrid(np.arange(8), np.arange(8), np.arange(4), indexing="ij")
    owners = np.stack([y // 4, (z * 4 + x) * 4 + y % 4], -1).reshape(-1, 2)
    return owners[np.random.RandomState(SEED).permutation(2 * CH)]


OWNERS = listing()
PLACE = np.zeros((2, CH), np.int64)
PLACE[OWNERS[:, 0], OWNERS[:, 1]] = np.arange(2 * CH)


def groups():
    yhi, station = OWNERS[:, 0], OWNERS[:, 1]
    return [[int(p) for p in (station * 2 + yhi) * 2 + core] for core in range(2)]


def dft_tables():
    phase = (np.arange(CH)[:, None] + OFFSET) * np.arange(FRAME)[None, :] % FRAME
    angle = phase * (2.0 * math.pi / FRAME)
    table = np.concatenate([np.cos(angle), -np.sin(angle)], 0) / math.sqrt(FRAME)
    high = table.astype(jnp.bfloat16)
    low = (table - high.astype(np.float64)).astype(jnp.bfloat16)
    return high, low


def dot_t(a, b):
    return lax.dot_general(a, b, (((1,), (1,)), ((), ())), preferred_element_type=jnp.float32)


def lane_ids(rows):
    return lax.broadcasted_iota(jnp.int32, (rows, LANES), 1)


def fetch(pairs, sems):
    copies = [pltpu.make_async_copy(src, dst, sems.at[n]) for n, (src, dst) in enumerate(pairs)]
    for copy in copies:
        copy.start()
    return copies


def run_filter(taps_ref, frame_at, keep, count, block):
    lo = block * LANES if isinstance(block, int) else pl.multiple_of(block * LANES, LANES)
    taps = [jnp.broadcast_to(taps_ref[k : k + 1, pl.ds(lo, LANES)], (N_IN, LANES)) for k in range(TAPS)]
    window = []
    for t in range(count + MARGIN):
        window.append(frame_at(t, lo).astype(jnp.float32))
        if t < MARGIN:
            continue
        total = taps[0] * window[0]
        for k in range(1, TAPS):
            total = total + taps[k] * window[k]
        window.pop(0)
        keep(t - MARGIN, total)


def pieces(x):
    high = x.astype(jnp.bfloat16)
    return high, (x - high.astype(jnp.float32)).astype(jnp.bfloat16)


def at(t, lo):
    if isinstance(lo, int):
        return slice(t * FRAME + lo, t * FRAME + lo + LANES)
    return pl.ds(pl.multiple_of(t * FRAME + lo, LANES), LANES)


def prefilter_kernel(
    volt_hbm, taps_hbm, high_hbm, low_hbm, fhigh, flow, seam, taps_ref, high_ref, low_ref, frames, filt, sems
):
    core, yhi = lax.axis_index("core"), lax.axis_index("yhi")
    edge = MARGIN * FRAME
    own = N_FR * FRAME
    nothing = jnp.zeros((N_IN, edge), jnp.bfloat16)
    offset = pl.multiple_of((1 - core) * edge, LANES)
    copies = fetch(
        [
            (volt_hbm, frames.at[:, pl.ds(offset, own)]),
            (taps_hbm, taps_ref),
            (high_hbm, high_ref),
            (low_hbm, low_ref),
        ],
        sems,
    )
    tail = pltpu.make_async_copy(volt_hbm.at[:, pl.ds(own - edge, edge)], frames.at[:, pl.ds(own, edge)], sems.at[4])
    second = (core == 1) & (yhi == 0)

    @pl.when(second)
    def _():
        tail.start()

    @pl.when(core == 0)
    def _():
        frames[:, :edge] = nothing

    @pl.when((core == 1) & (yhi == 1))
    def _():
        frames[:, own:] = nothing

    copies[0].wait()
    copies[1].wait()

    @pl.when(second)
    def _():
        tail.wait()

    seam[...] = frames[:, own:]

    for block in range(FRAME // LANES):
        def keep(f, x, block=block):
            filt[block, f * N_IN : (f + 1) * N_IN, :] = x

        run_filter(taps_ref, lambda t, lo: frames[:, at(t, lo)], keep, N_FR, block)

    for i in range(N_IN):
        for block in range(FRAME // LANES):
            high, low = pieces(filt[block, pl.ds(i, N_FR, stride=N_IN), :])
            fhigh[i * N_FR : (i + 1) * N_FR, block * LANES : (block + 1) * LANES] = high
            flow[i * N_FR : (i + 1) * N_FR, block * LANES : (block + 1) * LANES] = low
    copies[2].wait()
    copies[3].wait()


def channelize_kernel(fhigh, flow, seam, other_ref, taps_ref, high_ref, low_ref, out_ref, filt, ghigh, glow, spread):
    core, yhi = lax.axis_index("core"), lax.axis_index("yhi")
    more = HALF - N_FR
    real_samples = (core == 0) | (yhi == 1)

    def frame_at(t, lo):
        if t < MARGIN:
            return seam[:, at(t, lo)]
        return jnp.where(real_samples, other_ref[:, at(t - MARGIN, lo)].astype(jnp.float32), 0.0)

    for block in range(FRAME // LANES):
        def keep(f, x, block=block):
            filt[block, f * N_IN : (f + 1) * N_IN, :] = x

        run_filter(taps_ref, frame_at, keep, MARGIN, block)
        filt[block, MARGIN * N_IN :, :] = jnp.zeros(((more - MARGIN) * N_IN, LANES), jnp.float32)

    for i in range(N_IN):
        for block in range(FRAME // LANES):
            high, low = pieces(filt[block, pl.ds(i, more, stride=N_IN), :])
            ghigh[i * more : (i + 1) * more, block * LANES : (block + 1) * LANES] = high
            glow[i * more : (i + 1) * more, block * LANES : (block + 1) * LANES] = low

    lanes = lane_ids(CH)
    slot = lanes % HALF
    drop = (slot < MARGIN) & (core == 0) & (yhi == 1)
    split = (slot >= LOW_SLOT) & (slot < HIGH_SLOT) & (core == 1)

    def rows_of(f, g, i):
        return [f[i * N_FR : (i + 1) * N_FR, :], g[i * more : (i + 1) * more, :]]

    for pair in range(N_IN // 2):
        i = pair * 2
        fh = jnp.concatenate(rows_of(fhigh, ghigh, i) + rows_of(fhigh, ghigh, i + 1), 0)
        fl = jnp.concatenate(rows_of(flow, glow, i) + rows_of(flow, glow, i + 1), 0)
        spec = dot_t(high_ref[...], fh) + (dot_t(high_ref[...], fl) + dot_t(low_ref[...], fh))
        real, imag = spec[:CH], spec[CH:]
        first = jnp.where(lanes < HALF, real, pltpu.roll(imag, HALF, 1))
        second = jnp.where(lanes < HALF, pltpu.roll(real, HALF, 1), imag)
        for sub, value in enumerate((first, second)):
            rest = value - value.astype(jnp.bfloat16).astype(jnp.float32)
            value = jnp.where(split, pltpu.roll(rest, LANES - MARGIN, 1), value)
            value = jnp.where(drop, 0.0, value)
            spread[pl.ds(i + sub, CH, stride=N_IN), :] = value
    for pair in range(CH):
        two = [spread[int(c) * N_IN : (int(c) + 1) * N_IN, :] for c in OWNERS[2 * pair : 2 * pair + 2, 1]]
        out_ref[pair * 2 * N_IN : (pair + 1) * 2 * N_IN, :] = jnp.concatenate(two, 0).astype(jnp.bfloat16)


def two_tiles(in_ref, yhi, pair):
    tiles = []
    for place in PLACE[yhi, 2 * pair : 2 * pair + 2]:
        both = in_ref[int(place) // 2 * 2 * N_IN : (int(place) // 2 + 1) * 2 * N_IN, :].astype(jnp.float32)
        tiles.append(both[int(place) % 2 * N_IN : (int(place) % 2 + 1) * N_IN])
    return jnp.concatenate(tiles, 0)


def lay(in_ref, cols_ref, rows_ref, parts):
    core, yhi = lax.axis_index("core"), lax.axis_index("yhi")
    rows = rows_ref.shape[1]
    step = 2 * N_IN

    @pl.when(jnp.logical_not(parts))
    def _():
        for pair in range(CH // 2):
            for t in range(2):
                value = two_tiles(in_ref, t, pair).astype(jnp.bfloat16)
                cols_ref[pair * step : (pair + 1) * step, t * LANES : (t + 1) * LANES] = value

    @pl.when(parts)
    def _():
        slot = lane_ids(step) % HALF
        edge = (slot >= HIGH_SLOT) & (slot < SLOTS)
        low = (slot >= LOW_SLOT) & (slot < HIGH_SLOT)
        for pair in range(CH // 2):
            a, b = two_tiles(in_ref, 0, pair), two_tiles(in_ref, 1, pair)
            total = (a + pltpu.roll(a, MARGIN, 1)) + (b + pltpu.roll(b, MARGIN, 1))
            one = jnp.where(edge, total, jnp.where(low, 0.0, a))
            two = jnp.where(edge | low, 0.0, b)
            cut = slice(pair * step, (pair + 1) * step)
            cols_ref[cut, :LANES] = one.astype(jnp.bfloat16)
            cols_ref[cut, LANES:] = two.astype(jnp.bfloat16)

    own = pl.multiple_of((yhi * 2 + core) * rows, rows)
    lanes = lane_ids(rows)
    for t in range(2):
        x = cols_ref[pl.ds(own, rows), t * LANES : (t + 1) * LANES]
        rows_ref[0, :, t * LANES : (t + 1) * LANES] = x
        turned = pltpu.roll(x.astype(jnp.float32), HALF, 1)
        turned = jnp.where(lanes < HALF, turned, -turned)
        rows_ref[1, :, t * LANES : (t + 1) * LANES] = turned.astype(jnp.bfloat16)


def first_half_kernel(in_ref, part_ref, cols_ref, rows_ref):
    lay(in_ref, cols_ref, rows_ref, lax.axis_index("core") == 1)
    cols = part_ref.shape[3]
    for j in range(part_ref.shape[0]):
        for part in range(2):
            part_ref[j, part] = dot_t(rows_ref[part], cols_ref[j * cols : (j + 1) * cols, :])


def second_half_kernel(scale, in_ref, part_ref, out_hbm, cols_ref, rows_ref, out_ref, sems):
    lay(in_ref, cols_ref, rows_ref, lax.axis_index("core") == 0)
    chunks, _, _, cols = out_ref.shape
    copies = []
    for j in range(chunks):
        cut = slice(j * cols, (j + 1) * cols)
        for part in range(2):
            out_ref[j, part] = (part_ref[j, part] + dot_t(rows_ref[part], cols_ref[cut, :])) * scale
            copy = pltpu.make_async_copy(out_ref.at[j, part], out_hbm.at[part, 0, :, cut], sems.at[j, part])
            copy.start()
            copies.append(copy)
    for copy in copies:
        copy.wait()


def far_memory(x):
    return pltpu.with_memory_space_constraint(x, pltpu.HBM)


def per_device(voltages, fir_taps):
    other = lax.ppermute(voltages, "core", SWAP)
    high, low = (jnp.asarray(table) for table in dft_tables())
    seam_shape = (N_IN, MARGIN * FRAME)
    fhigh, flow, seam, taps, high, low = pl.pallas_call(
        prefilter_kernel,
        out_shape=[
            jax.ShapeDtypeStruct((N_IN * N_FR, FRAME), jnp.bfloat16),
            jax.ShapeDtypeStruct((N_IN * N_FR, FRAME), jnp.bfloat16),
            jax.ShapeDtypeStruct(seam_shape, jnp.bfloat16),
            jax.ShapeDtypeStruct(fir_taps.shape, jnp.float32),
            jax.ShapeDtypeStruct(high.shape, jnp.bfloat16),
            jax.ShapeDtypeStruct(low.shape, jnp.bfloat16),
        ],
        in_specs=[HBM] * 4,
        out_specs=[VMEM] * 6,
        scratch_shapes=[
            pltpu.VMEM((N_IN, SLOTS * FRAME), jnp.bfloat16),
            pltpu.VMEM((FRAME // LANES, N_FR * N_IN, LANES), jnp.float32),
            pltpu.SemaphoreType.DMA((5,)),
        ],
        compiler_params=PARAMS,
        cost_estimate=pl.CostEstimate(flops=10**8, bytes_accessed=4 * 10**6, transcendentals=0),
        name="prefilter",
    )(*(far_memory(x) for x in (voltages, fir_taps, high, low)))
    more = HALF - N_FR
    spectra = pl.pallas_call(
        channelize_kernel,
        out_shape=jax.ShapeDtypeStruct((2 * CH * N_IN, LANES), jnp.bfloat16),
        in_specs=[VMEM] * 7,
        out_specs=VMEM,
        scratch_shapes=[
            pltpu.VMEM((FRAME // LANES, more * N_IN, LANES), jnp.float32),
            pltpu.VMEM((more * N_IN, FRAME), jnp.bfloat16),
            pltpu.VMEM((more * N_IN, FRAME), jnp.bfloat16),
            pltpu.VMEM((CH * N_IN, LANES), jnp.float32),
        ],
        compiler_params=PARAMS,
        name="channelize",
    )(fhigh, flow, seam, other, taps, high, low)
    turned = lax.all_to_all(
        spectra.reshape(2 * CH, N_IN, LANES), AXES, 0, 0, axis_index_groups=groups(), tiled=True
    )
    own = turned.reshape(2 * N_INPUTS, LANES)
    other_core = lax.ppermute(own, "core", SWAP)
    rows = N_INPUTS // N_TB
    cols = 512
    chunks = N_INPUTS // cols
    operands = [
        pltpu.VMEM((N_INPUTS, 2 * LANES), jnp.bfloat16),
        pltpu.VMEM((2, rows, 2 * LANES), jnp.bfloat16),
    ]
    half = pl.pallas_call(
        first_half_kernel,
        out_shape=jax.ShapeDtypeStruct((chunks, 2, rows, cols), jnp.float32),
        in_specs=[VMEM],
        out_specs=VMEM,
        scratch_shapes=operands,
        compiler_params=PARAMS,
        cost_estimate=pl.CostEstimate(flops=3 * 10**8, bytes_accessed=3 * 10**6, transcendentals=0),
        name="first_half",
    )(own)
    scale = np.float32(1.0 / (N_FR * N_TB))
    return pl.pallas_call(
        lambda *refs: second_half_kernel(scale, *refs),
        out_shape=jax.ShapeDtypeStruct((2, 1, rows, N_INPUTS), jnp.float32),
        in_specs=[VMEM, VMEM],
        out_specs=HBM,
        scratch_shapes=operands
        + [
            pltpu.VMEM((chunks, 2, rows, cols), jnp.float32),
            pltpu.SemaphoreType.DMA((chunks, 2)),
        ],
        compiler_params=PARAMS,
        name="second_half",
    )(other_core, half)


def solution(mesh):
    fine = Mesh(mesh.devices.reshape(SIZES), AXES)
    in_specs = (P(("z", "x", "ylo"), ("yhi", "core")), P())
    out_specs = P(None, ("z", "x", "ylo"), ("yhi", "core"), None)
    return jax.shard_map(
        per_device, mesh=fine, in_specs=in_specs, out_specs=out_specs, check_vma=False
    )
```
